512 devices in a mesh: gx: 32 (over x, z_lo, core), gy: 16 (over z_hi, y).
Axes of the slice: x: 4, y: 8, z: 8 (z_hi: 2, z_lo: 4; z = z_hi * 4 + z_lo), core: 2. Of those that a mesh axis runs over, the one named last changes fastest.
Arguments:
- features: bfloat16 [32, 512, 4096], P(None, 'gx', 'gy'), may hold values from -6 to 6
- brick_mask: int32 [32, 16, 1], P('gx', 'gy'), may hold values 0 or 1
- kernel_fine: bfloat16 [27, 1024], replicated, may hold values from -0.21875 to 0.21875
- kernel_down: bfloat16 [8, 2048], replicated, may hold values from -0.375 to 0.375
- kernel_coarse: bfloat16 [27, 4096], replicated, may hold values from -0.15625 to 0.15625
- cotangent: bfloat16 [64, 256, 1024], P(None, 'gx', 'gy'), may hold values from -24 to 24
Outputs:
- grad_features: bfloat16 [32, 512, 4096], P(None, 'gx', 'gy')
The draws below stay inside these ranges and needn't reach their ends.
All inputs are finite; a program needn't handle non-finite values. No bound on the sum of `brick_mask` on one device may be relied on, other than what follows from the above.
Results may differ from the reference program's by a relative error of at most 0.014.
Values may be sent and summed in bfloat16 or wider, within the bound.
No kernel may reach another device: no remote copies, remote signals or barrier semaphores. Data moves between devices by JAX's collectives and lax.ppermute only.
A program may use at most 64 MiB of HBM per device.

```python
import jax
import jax.numpy as jnp
from jax import lax

BRICK = 16
C1 = 32
C2 = 64
BZ = 1
NX = 512
NY = 256
NZ = 16


def place_ends(drawn, key, smallest, high):
    longest = drawn.shape.index(max(drawn.shape))
    spots = []
    for shift in (0, 1):
        where = [jax.random.randint(jax.random.fold_in(key, axis), (), 0, length) for axis, length in enumerate(drawn.shape)]
        where[longest] = (where[longest] + shift) % drawn.shape[longest]
        spots.append(tuple(where))
    return drawn.at[spots[0]].set(smallest).at[spots[1]].set(high)


def steps_of(own_key, extent, cuts, low, top_value):
    def one(dim, shards_of):
        heights = jax.random.uniform(jax.random.fold_in(jax.random.fold_in(own_key, 6), dim), (shards_of,), jnp.float32, low / len(cuts), top_value / len(cuts))
        return jnp.repeat(jnp.exp(heights), extent[dim] // shards_of).reshape((-1,) + (1,) * (len(extent) - dim - 1))

    factor_of = one(*cuts[0])
    for cut in cuts[1:]:
        factor_of = factor_of * one(*cut)
    return factor_of


def gaussian(own_key, extent, width, bound, cuts=(), kind=jnp.bfloat16):
    factor_of = steps_of(own_key, extent, cuts, -0.22, 0.18) if cuts else 1.0
    array = jax.random.normal(own_key, extent, jnp.float32) * width * factor_of
    return jnp.minimum(jnp.maximum(array, -bound), bound).astype(kind)


def setup_inputs(seed: int = 0) -> dict:
    keys = jax.random.split(jax.random.key(seed), 7)
    return {
        "features": gaussian(keys[0], (C1, NX, NY * NZ), 1.0, 6.0, ((1, 32), (2, 16))),
        "brick_mask": place_ends((jax.random.randint(keys[1], (NX // BRICK, NY // BRICK, BZ), 0, 4) < 3).astype(jnp.int32), jax.random.fold_in(keys[1], 1), 0, 1),
        "kernel_fine": gaussian(keys[2], (27, C1 * C1), (27 * C1) ** -0.5, 0.21875),
        "kernel_down": gaussian(keys[3], (8, C2 * C1), (8 * C1) ** -0.5, 0.375),
        "kernel_coarse": gaussian(keys[4], (27, C2 * C2), (27 * C2) ** -0.5, 0.15625),
        "cotangent": gaussian(keys[5], (C2, NX // 2, NY * NZ // 4), 4.0, 24.0, ((1, 32), (2, 16))),
    }


exact_mode = lax.Precision.HIGHEST
layout = ("NCDHW", "OIDHW", "NCDHW")


def unpack_kernel(kernel, side, size_out, size_in):
    return kernel.reshape(side, side, side, size_out, size_in).transpose(3, 4, 0, 1, 2)


def conv_full(padded, kernel):
    return lax.conv_general_dilated(padded[None], kernel, (1, 1, 1), "VALID", dimension_numbers=layout, precision=exact_mode)[0]


def flipped(kernel):
    return jnp.flip(kernel, (2, 3, 4)).transpose(1, 0, 2, 3, 4)


def pad_all(volume):
    return jnp.pad(volume, ((0, 0), (1, 1), (1, 1), (1, 1)))


def reduce_down(field, kernel):
    return lax.conv_general_dilated(field.astype(jnp.float32)[None], kernel.astype(jnp.float32), (2, 2, 2), "VALID", dimension_numbers=layout, precision=exact_mode)[0]


def spread_up(gradient, kernel):
    product = jnp.einsum("ocabe,oxyz->cxaybze", kernel.astype(jnp.float32), gradient.astype(jnp.float32), precision=exact_mode)
    shape = product.shape
    return product.reshape(shape[0], shape[1] * 2, shape[3] * 2, shape[5] * 2)


def derivative(value):
    logistic = jax.nn.sigmoid(value)
    return logistic * (1.0 + value * (1.0 - logistic))


def brick_cells(flags, repeat_by):
    grown = jnp.repeat(jnp.repeat(jnp.repeat(flags, repeat_by, 0), repeat_by, 1), repeat_by, 2)
    return grown.astype(jnp.float32)


def reference(features, brick_mask, kernel_fine, kernel_down, kernel_coarse, cotangent):
    features = features.reshape(C1, NX, NY, NZ)
    cotangent = cotangent.reshape(C2, NX // 2, NY // 2, NZ // 2)
    kernel_fine = unpack_kernel(kernel_fine, 3, C1, C1)
    kernel_down = unpack_kernel(kernel_down, 2, C2, C1)
    kernel_coarse = unpack_kernel(kernel_coarse, 3, C2, C2)
    block_rows = BRICK
    block_count = NX // BRICK
    fine_flags = brick_cells(brick_mask, BRICK)
    coarse_flags = brick_cells(brick_mask, BRICK // 2)
    kernel_one = kernel_fine.astype(jnp.float32)
    kernel_two = kernel_coarse.astype(jnp.float32)
    padded = pad_all(features)
    indices = jnp.arange(block_count, dtype=jnp.int32)

    def first_conv(start_row):
        piece = lax.dynamic_slice_in_dim(padded, start_row, block_rows + 2, 1).astype(jnp.float32)
        return conv_full(piece, kernel_one)

    def forward_block(block_index):
        start_row = block_index * block_rows
        pre_fine = first_conv(start_row)
        flag_rows = lax.dynamic_slice_in_dim(fine_flags, start_row, block_rows, 0)
        hidden = (flag_rows * jax.nn.silu(pre_fine)).astype(jnp.bfloat16)
        return reduce_down(hidden, kernel_down).astype(jnp.bfloat16)

    pieces = lax.map(forward_block, indices)
    down_field = jnp.moveaxis(pieces, 0, 1).reshape(C2, NX // 2, NY // 2, NZ // 2)
    pre_coarse = conv_full(pad_all(down_field).astype(jnp.float32), kernel_two)
    grad_coarse = (cotangent.astype(jnp.float32) * coarse_flags * derivative(pre_coarse)).astype(jnp.bfloat16)
    grad_down = conv_full(pad_all(grad_coarse).astype(jnp.float32), flipped(kernel_two)).astype(jnp.bfloat16)

    def backward_block(block_index):
        start_row = block_index * block_rows
        pre_fine = first_conv(start_row)
        flag_rows = lax.dynamic_slice_in_dim(fine_flags, start_row, block_rows, 0)
        coarse_rows = lax.dynamic_slice_in_dim(grad_down, start_row // 2, block_rows // 2, 1)
        return (spread_up(coarse_rows, kernel_down) * flag_rows * derivative(pre_fine)).astype(jnp.bfloat16)

    pieces_back = lax.map(backward_block, indices)
    grad_fine = jnp.moveaxis(pieces_back, 0, 1).reshape(C1, NX, NY, NZ)
    grad_padded = pad_all(grad_fine)
    kernel_back = flipped(kernel_one)

    def last_block(block_index):
        start_row = block_index * block_rows
        piece = lax.dynamic_slice_in_dim(grad_padded, start_row, block_rows + 2, 1).astype(jnp.float32)
        return conv_full(piece, kernel_back).astype(jnp.bfloat16)

    pieces_last = lax.map(last_block, indices)
    return jnp.moveaxis(pieces_last, 0, 1).reshape(C1, NX, NY * NZ)
```

```python
import jax
import jax.numpy as jnp
from jax import lax
from jax.experimental import pallas as pl
from jax.experimental.pallas import tpu as pltpu
from jax.sharding import PartitionSpec as P

C1 = 32
C2 = 64
LANES = 256
HALO = 4
NB = 8
WIDE = NB + 2 * HALO
YMSG = NB * HALO * NB + 32 + 16
XMSG = 192 + 48 + 16 + 64
F32 = jnp.float32
BF16 = jnp.bfloat16
NT = (((1,), (1,)), ((), ()))
TN = (((0,), (0,)), ((), ()))


def iota(shape, dim):
    return lax.broadcasted_iota(jnp.int32, shape, dim)


def one_hot(cond):
    return jnp.where(cond, 1.0, 0.0).astype(BF16)


def dot(a, b):
    return jnp.dot(a, b, preferred_element_type=F32)


def block_sum_matrix():
    r, l = iota((64, 256), 0), iota((64, 256), 1)
    return one_hot((r // 8 == l // 32) & (r % 8 == (l % 16) // 2))


def parity_matrix():
    r, l = iota((256, 256), 0), iota((256, 256), 1)
    return one_hot(((r // 64) % 2 == (l // 16) % 2) & ((r // 32) % 2 == l % 2))


def is_odd(axis):
    return lax.rem(lax.axis_index(axis), 2)


def pack_kernel(flag_ref, feat_ref, own_ref, first_ref, second_ref, f_scr):
    odd = is_odd("gy")
    marks = jnp.full((16, LANES), flag_ref[0].astype(F32), F32).astype(BF16)
    q = block_sum_matrix()
    parity = parity_matrix()
    cells = feat_ref[...].astype(F32).reshape(512, 256)
    f_scr[0] = cells[:, :128]
    f_scr[1] = cells[:, 128:]
    for xb in range(NB):
        parts = []
        for a0 in range(2):
            at = pl.ds(2 * xb + a0, C1, stride=16)
            rows = jnp.concatenate([f_scr[0, at, :], f_scr[1, at, :]], axis=1).astype(BF16)
            parts += [rows] * 4
        spread = jnp.concatenate(parts, axis=0) * parity
        own_ref[xb] = lax.dot_general(q, spread, NT, preferred_element_type=F32).astype(BF16)
    for ref, side in ((first_ref, odd), (second_ref, 1 - odd)):
        for xb in range(NB):
            ref[pl.ds(xb * 32, 32), :] = own_ref[xb, pl.ds(pl.multiple_of(32 * side, 32), 32), :]
        ref[pl.ds(288, 16), :] = marks


def pack_cot_kernel(flag_ref, cot_ref, first_in, second_in, cown_ref, first_ref, second_ref, c_scr):
    odd = is_odd("gy")
    for ref, features in ((first_ref, first_in), (second_ref, second_in)):
        ref[pl.ds(0, 256), :] = features[pl.ds(0, 256), :]
        ref[pl.ds(288, 16), :] = features[pl.ds(288, 16), :]
    eye = one_hot(iota((64, 64), 0) == iota((64, 64), 1))
    c_scr[:, :64] = cot_ref[...].astype(F32).reshape(512, 64) * flag_ref[0].astype(F32)
    for p in range(4):
        rows = jnp.concatenate(
            [c_scr[pl.ds(2 * p + b, C2, stride=8), :] for b in range(2)], axis=0
        )[:, :64].astype(BF16)
        cown_ref[p] = lax.dot_general(eye, rows, NT, preferred_element_type=F32).astype(BF16)
    for ref, side in ((first_ref, odd), (second_ref, 1 - odd)):
        for p in range(4):
            at = (pl.ds(256 + 16 * (p // 2), 16), pl.ds(128 * (p % 2), 128))
            ref[at] = cown_ref[p, pl.ds(pl.multiple_of(48 * side, 16), 16), :]


OFFSETS = {(0, 0): 0, (1, 0): 1, (0, 1): 2, (1, 1): -1}


def fine_weights(u_ref, out_ref, u_scr, v_scr, w_scr, backward):
    tile = one_hot(iota((32, 256), 0) == iota((32, 256), 1) % 32)
    u_scr[...] = dot(u_ref[...], tile).astype(BF16).reshape(27, 32, 256)
    lane = iota((32, 256), 1)
    low2 = one_hot((lane // 32) % 2 == 0), one_hot((lane // 32) % 2 == 1)
    low1 = one_hot((lane // 64) % 2 == 0), one_hot((lane // 64) % 2 == 1)

    def taps(f):
        return ((-f, 1 - f) if backward else (f, f - 1))

    def mix(load, f, masks):
        terms = [load(e) * mask for e, mask in zip(taps(f), masks) if abs(e) <= 1]
        return sum(terms[1:], terms[0])

    def body(e0, carry):
        for e1 in range(3):
            for f2 in range(-1, 3):
                v_scr[e0 * 12 + e1 * 4 + (f2 + 1)] = mix(
                    lambda e2: u_scr[e0 * 9 + e1 * 3 + e2 + 1], f2, low2
                )
        for f1 in range(-1, 3):
            for f2 in range(-1, 3):
                w_scr[e0 * 16 + (f1 + 1) * 4 + f2 + 1] = mix(
                    lambda e1: v_scr[e0 * 12 + (e1 + 1) * 4 + f2 + 1], f1, low1
                )
        return carry

    lax.fori_loop(0, 3, body, 0)
    half = jnp.zeros((32, 128), BF16)
    for my in range(2):
        for mz in range(2):
            for mx in range(2):
                for a0 in range(2):
                    for a1 in range(2):
                        for a2 in range(2):
                            f0, f1, f2 = OFFSETS[a0, mx], OFFSETS[a1, my], OFFSETS[a2, mz]
                            row = ((my * 2 + mz) * 2 + mx) * 256 + (a0 * 4 + a1 * 2 + a2) * 32
                            for b0, e0 in enumerate(taps(f0)):
                                at = (pl.ds(row, 32), pl.ds(128 * b0, 128))
                                if abs(e0) <= 1:
                                    out_ref[at] = w_scr[(e0 + 1) * 16 + (f1 + 1) * 4 + f2 + 1, :, 128 * b0 : 128 * b0 + 128]
                                else:
                                    out_ref[at] = half


def coarse_weights(u_ref, out_ref, u_scr, backward):
    if backward:
        tile = one_hot(iota((64, 128), 0) == iota((64, 128), 1) % 64)
        u_scr[...] = dot(u_ref[...], tile).astype(BF16).reshape(27, 64, 128)
    else:
        eye = one_hot(iota((64, 64), 0) == iota((64, 64), 1))
        for e in range(27):
            turned = lax.dot_general(eye, u_ref[pl.ds(64 * e, 64), :], NT, preferred_element_type=F32)
            u_scr[e] = jnp.concatenate([turned, turned], axis=1).astype(BF16)
    masks = one_hot(iota((64, 128), 1) < 64), one_hot(iota((64, 128), 1) >= 64)

    def body(t, carry):
        k = 8 - t if backward else t
        for s in range(4):
            taps = (1 - s, 2 - s) if backward else (s - 1, s - 2)
            terms = [u_scr[(e + 1) * 9 + k] * mask for e, mask in zip(taps, masks) if abs(e) <= 1]
            out_ref[pl.ds(t * 256 + s * 64, 64), :] = sum(terms[1:], terms[0])
        return carry

    lax.fori_loop(0, 9, body, 0)


def weight_kernel(
    u1_ref, u1b_ref, u2_ref, kd_ref, ku_ref,
    w1_ref, w2_ref, w3_ref, w4_ref, wd_ref, wu_ref,
    u_scr, v_scr, w_scr, uc_scr,
):
    fine_weights(u1_ref, w1_ref, u_scr, v_scr, w_scr, False)
    fine_weights(u1b_ref, w2_ref, u_scr, v_scr, w_scr, True)
    coarse_weights(u2_ref, w3_ref, uc_scr, False)
    coarse_weights(u2_ref, w4_ref, uc_scr, True)
    for b in range(2):
        place = one_hot(iota((64, 128), 0) + 64 * b == iota((64, 128), 1))
        wd_ref[pl.ds(256 * b, 256), :] = dot(kd_ref[...], place).astype(BF16)
        zero = jnp.zeros((64, 256), BF16)
        wu_ref[b, pl.ds(64 * b, 64), :] = ku_ref[...]
        wu_ref[b, pl.ds(64 * (1 - b), 64), :] = zero


def silu_parts(v):
    s = 0.5 + 0.5 * jnp.tanh(0.5 * v)
    vs = v * s
    return vs, s + vs * (1.0 - s)


def shift_z(cells, up):
    z = iota(cells.shape, 1)
    if up:
        return jnp.where(z < 7, pltpu.roll(cells, 7, 1), 0.0)
    return jnp.where(z > 0, pltpu.roll(cells, 1, 1), 0.0)


def mixed(cells, store):
    n = cells.shape[0]
    rows = (n - 2) * 8
    lane = iota(cells.shape, 2)
    zmix = jnp.where((lane // 32) % 2 == 0, shift_z(cells, True), shift_z(cells, False))
    low1 = (iota((n - 2, 8, 256), 2) // 64) % 2 == 0
    for mz, form in enumerate((cells, zmix)):
        store(mz, form[1 : n - 1].reshape(rows, 256).astype(BF16))
        store(2 + mz, jnp.where(low1, form[2:], form[: n - 2]).reshape(rows, 256).astype(BF16))


def conv_lhs(before, here, after):
    parts = []
    for m in range(4):
        parts += [here[0][m, here[1]], after[0][m, after[1], :, :128], before[0][m, before[1], :, 128:]]
    return jnp.concatenate(parts, axis=1)


def coarse_forms(cells, store):
    n = cells.shape[0]
    for dz, form in enumerate((shift_z(cells, False), cells, shift_z(cells, True))):
        for dy in range(3):
            store(dy * 3 + dz, form[dy : dy + n - 2].reshape((n - 2) * 8, 128).astype(BF16))


def storer(scr, slot):
    def store(m, value):
        scr[m, slot] = value

    return store


def pair_lhs(low, high):
    parts = []
    for t in range(9):
        parts += [low[0][t, low[1]], high[0][t, high[1]]]
    return jnp.concatenate(parts, axis=1)


def spread_block(p_scr, slot, cells):
    mixed(cells.astype(F32).reshape(16, 8, 256), storer(p_scr, slot))


def forward_pair(places, marks, w1_ref, wd_ref, dv_scr, dv_slot, d_scr, d_slot):
    lhs = jnp.concatenate([conv_lhs(*places[:3]), conv_lhs(*places[1:])], axis=0)
    pre = dot(lhs, w1_ref[...])
    hidden = []
    for b in range(2):
        value, slope = silu_parts(pre[112 * b : 112 * b + 112])
        flags = jnp.concatenate([marks(b)] * 2, axis=1)
        hidden.append((flags * value).astype(BF16))
        dv_scr[dv_slot + b] = (flags * slope)[16:96]
    down = dot(jnp.concatenate(hidden, axis=1), wd_ref[...]).astype(BF16)
    coarse_forms(down.astype(F32).reshape(14, 8, 128), storer(d_scr, d_slot))
    return down


def coarse_forward(places, cots, w3_ref, g_scr, g_first):
    lhs = jnp.concatenate([pair_lhs(*places[:2]), pair_lhs(*places[1:])], axis=0)
    pre = dot(lhs, w3_ref[...])
    for k in range(2):
        _, slope = silu_parts(pre[96 * k : 96 * k + 96])
        grad = (cots(k).astype(F32) * slope).astype(BF16)
        coarse_forms(grad.astype(F32).reshape(12, 8, 128), storer(g_scr, g_first + k))


def fine_gradient(grad, slopes, wu_ref, q_scr, slot):
    for b in range(2):
        fine = (dot(grad, wu_ref[b]) * slopes(b)).astype(BF16)
        mixed(fine.astype(F32).reshape(10, 8, 256), storer(q_scr, slot + b))


def edge_kernel(
    flag_ref, own_ref, cown_ref, ya_ref, yb_ref, w1_ref, wd_ref,
    first_ref, second_ref, cot_ref, marks_ref, p_ref, dv_ref, d_ref,
    ext_ref, down_scr,
):
    odd_y, odd_x = is_odd("gy"), is_odd("gx")

    def place(above, below):
        for xb in range(NB):
            ext_ref[xb, pl.ds(0, 32), :] = above[pl.ds(xb * 32, 32), :]
            ext_ref[xb, pl.ds(32, 64), :] = own_ref[xb]
            ext_ref[xb, pl.ds(96, 32), :] = below[pl.ds(xb * 32, 32), :]
        for p in range(4):
            at = (pl.ds(256 + 16 * (p // 2), 16), pl.ds(128 * (p % 2), 128))
            cot_ref[p, pl.ds(0, 16), :] = above[at]
            cot_ref[p, pl.ds(16, 64), :] = cown_ref[p]
            cot_ref[p, pl.ds(80, 16), :] = below[at]
        for k in range(2):
            marks_ref[pl.ds(16 * k, 16), :] = above[pl.ds(288, 16), pl.ds(0, 128)]
            marks_ref[pl.ds(96 + 16 * k, 16), :] = below[pl.ds(288, 16), pl.ds(0, 128)]

    marks_ref[pl.ds(32, 64), :] = jnp.full((64, 128), flag_ref[0].astype(F32), F32).astype(BF16)
    pl.when(odd_y == 1)(lambda: place(yb_ref, ya_ref))
    pl.when(odd_y == 0)(lambda: place(ya_ref, yb_ref))

    marks = marks_ref[...].astype(F32)[8:120]
    for k in range(NB):
        spread_block(p_ref, k, ext_ref[k])
    for n in range(2):
        places = [(p_ref, 4 * n + k) for k in range(4)]
        down_scr[n] = forward_pair(places, lambda b: marks, w1_ref, wd_ref, dv_ref, 2 * n, d_ref, n)

    def send(low, high):
        for ref, n, near, outer, lane in ((low, 0, 0, 1, 0), (high, 1, 7, 6, 128)):
            ref[pl.ds(0, 128), :] = ext_ref[near]
            for h in range(2):
                half = pl.ds(128 * h, 128)
                ref[pl.ds(128, 64), half] = ext_ref[outer, pl.ds(64 * h, 64), pl.ds(lane, 128)]
                ref[pl.ds(192, 48), half] = cot_ref[3 * n, pl.ds(48 * h, 48), :]
            ends = [marks_ref[pl.ds(96 * k, 16), :].astype(F32)[:8] for k in range(2)]
            ref[pl.ds(240, 16), pl.ds(0, 128)] = jnp.concatenate(ends, axis=0).astype(BF16)
            ref[pl.ds(240, 16), pl.ds(128, 128)] = marks_ref[pl.ds(32, 16), :]
            ref[pl.ds(256, 64), pl.ds(0, 128)] = down_scr[n, pl.ds(0, 64), :]
            ref[pl.ds(256, 48), pl.ds(128, 128)] = down_scr[n, pl.ds(64, 48), :]
            ref[pl.ds(304, 16), pl.ds(128, 128)] = jnp.zeros((16, 128), BF16)

    pl.when(odd_x == 1)(lambda: send(second_ref, first_ref))
    pl.when(odd_x == 0)(lambda: send(first_ref, second_ref))


def middle_kernel(
    cot_ref, marks_ref, p_ref, d_ref, w1_ref, w3_ref, w4_ref, wd_ref, wu_ref,
    g_ref, q_ref,
    dv_scr, d_scr,
):
    marks = marks_ref[...].astype(F32)[8:120]
    places = [(p_ref, 2 + k) for k in range(4)]
    forward_pair(places, lambda b: marks, w1_ref, wd_ref, dv_scr, 0, d_scr, 0)
    places = [(d_ref, 0), (d_scr, 0), (d_ref, 1)]
    coarse_forward(places, lambda k: cot_ref[1 + k], w3_ref, g_ref, 0)
    grad = dot(pair_lhs((g_ref, 0), (g_ref, 1)), w4_ref[...]).astype(BF16)
    fine_gradient(grad, lambda b: dv_scr[b], wu_ref, q_ref, 0)


def main_kernel(
    cot_ref, marks_ref, xa_ref, xb_ref, pe_ref, dve_ref, de_ref, gm_ref, qm_ref,
    w1_ref, w2_ref, w3_ref, w4_ref, wd_ref, wu_ref,
    out_ref,
    p_scr, flag_scr, dv_scr, d_scr, cot_scr, g_scr, q_scr, o_scr,
):
    odd = is_odd("gx")

    def receive(left_ref, right_ref):
        sides = ((left_ref, 0, 0, 0, 1, 0, 128), (right_ref, 2, 3, 3, 2, 3, 0))
        for ref, flag_slot, cot_slot, d_slot, near, outer, lane in sides:
            ends = ref[pl.ds(240, 16), pl.ds(0, 128)].astype(F32)
            own = ref[pl.ds(240, 16), pl.ds(128, 128)].astype(F32)
            flag_scr[flag_slot] = jnp.concatenate([ends[:8]] * 3 + [own] * 4 + [ends[8:]] * 3, axis=0)
            for h in range(2):
                cot_scr[cot_slot, pl.ds(48 * h, 48), :] = ref[pl.ds(192, 48), pl.ds(128 * h, 128)]
            down = [ref[pl.ds(256, 64 - 16 * h), pl.ds(128 * h, 128)] for h in range(2)]
            down = jnp.concatenate(down, axis=0).astype(F32)
            coarse_forms(down.reshape(14, 8, 128), storer(d_scr, d_slot))
            spread_block(p_scr, near, ref[pl.ds(0, 128), :])
            half = jnp.concatenate([ref[pl.ds(128, 64), pl.ds(128 * h, 128)] for h in range(2)], axis=0)
            zero = jnp.zeros((128, 128), BF16)
            spread_block(p_scr, outer, jnp.concatenate([half, zero] if lane == 0 else [zero, half], axis=1))

    pl.when(odd == 1)(lambda: receive(xb_ref, xa_ref))
    pl.when(odd == 0)(lambda: receive(xa_ref, xb_ref))
    flag_scr[1] = marks_ref[...].astype(F32)[8:120]
    cot_scr[1] = cot_ref[0]
    cot_scr[2] = cot_ref[3]
    for m in range(4):
        for k in range(2):
            q_scr[m, 4 + k] = qm_ref[m, k]

    left = [(p_scr, 0), (p_scr, 1), (pe_ref, 0), (pe_ref, 1)]
    right = [(pe_ref, 6), (pe_ref, 7), (p_scr, 2), (p_scr, 3)]
    for n, (places, regions) in enumerate(((left, (0, 1)), (right, (1, 2)))):
        forward_pair(places, lambda b: flag_scr[regions[b]], w1_ref, wd_ref, dv_scr, 2 * n, d_scr, 1 + n)

    coarse_forward([(d_scr, 0), (d_scr, 1), (de_ref, 0)], lambda k: cot_scr[k], w3_ref, g_scr, 0)
    coarse_forward([(de_ref, 1), (d_scr, 2), (d_scr, 3)], lambda k: cot_scr[2 + k], w3_ref, g_scr, 2)

    left = [(g_scr, 0), (g_scr, 1), (gm_ref, 0)]
    right = [(gm_ref, 1), (g_scr, 2), (g_scr, 3)]
    slopes = [((dv_scr, 0), (dve_ref, 0)), ((dve_ref, 2), (dv_scr, 2))]
    for n, places in enumerate((left, right)):
        lhs = jnp.concatenate([pair_lhs(*places[:2]), pair_lhs(*places[1:])], axis=0)
        grad = dot(lhs, w4_ref[...]).astype(BF16)
        for k in range(2):
            ref, slot = slopes[n][k]
            fine_gradient(grad[80 * k : 80 * k + 80], lambda b: ref[slot + b], wu_ref, q_scr, 6 * n + 2 * k)

    q = block_sum_matrix()
    parity = parity_matrix().astype(F32)
    for h in range(2):
        lhs = jnp.concatenate(
            [conv_lhs(*((q_scr, 4 * h + k + n) for n in range(3))) for k in range(4)], axis=0
        )
        grad = dot(lhs, w2_ref[...]).astype(BF16)
        for k in range(4):
            spread = lax.dot_general(grad[64 * k : 64 * k + 64], q, TN, preferred_element_type=F32) * parity
            for b in range(2):
                rows = sum(spread[128 * b + 32 * i : 128 * b + 32 * i + 32] for i in range(4))
                at = pl.ds(8 * h + 2 * k + b, C1, stride=16)
                o_scr[0, at, :] = rows[:, :128]
                o_scr[1, at, :] = rows[:, 128:]
    cells = jnp.concatenate([o_scr[0], o_scr[1]], axis=1)
    out_ref[...] = cells.reshape(32, 16, 256).astype(BF16)


VMEM = pl.BlockSpec(memory_space=pltpu.VMEM)
SMEM = pl.BlockSpec(memory_space=pltpu.SMEM)


def call(kernel, specs, outs, scratch, flops, nbytes, *args):
    return pl.pallas_call(
        kernel,
        out_shape=outs,
        in_specs=specs,
        out_specs=jax.tree.map(lambda _: VMEM, outs),
        scratch_shapes=scratch,
        compiler_params=pltpu.CompilerParams(vmem_limit_bytes=24 * 1024 * 1024),
        cost_estimate=pl.CostEstimate(flops=flops, bytes_accessed=nbytes, transcendentals=0),
    )(*args)


def shape(*dims, dtype=BF16):
    return jax.ShapeDtypeStruct(dims, dtype)


def swaps(first, second, axis):
    count = lax.axis_size(axis)

    def both_ways(start):
        edges = [(i, i + 1) for i in range(start, count - 1, 2)]
        return edges + [(j, i) for i, j in edges]

    return lax.ppermute(first, axis, both_ways(1)), lax.ppermute(second, axis, both_ways(0))


def on_device(features, brick_mask, kernel_fine, kernel_down, kernel_coarse, cotangent):
    flag = brick_mask.reshape(1)
    own, y_first, y_second = call(
        pack_kernel,
        [SMEM, VMEM],
        [shape(8, 64, 256), shape(YMSG, 256), shape(YMSG, 256)],
        [pltpu.VMEM((2, 512, 128), F32)],
        2 * 10**9, 10**6, flag, features,
    )
    cown, y_first, y_second = call(
        pack_cot_kernel,
        [SMEM, VMEM, VMEM, VMEM],
        [shape(4, 64, 128), shape(YMSG, 256), shape(YMSG, 256)],
        [pltpu.VMEM((512, 128), F32)],
        10**9, 10**5, flag, cotangent, y_first, y_second,
    )
    y_a, y_b = swaps(y_first, y_second, "gy")
    fine = kernel_fine.reshape(27, C1, C1)
    down = kernel_down.reshape(8, C2, C1)
    w1, w2, w3, w4, wd, wu = call(
        weight_kernel,
        [VMEM] * 5,
        [shape(2048, 256), shape(2048, 256), shape(2304, 128), shape(2304, 128), shape(512, 128), shape(2, 128, 256)],
        [
            pltpu.VMEM((27, 32, 256), BF16),
            pltpu.VMEM((36, 32, 256), BF16),
            pltpu.VMEM((48, 32, 256), BF16),
            pltpu.VMEM((27, 64, 128), BF16),
        ],
        10**9, 10**7,
        fine.transpose(0, 2, 1).reshape(27 * C1, C1),
        fine.reshape(27 * C1, C1),
        kernel_coarse.reshape(27 * C2, C2),
        down.transpose(0, 2, 1).reshape(8 * C1, C2),
        down.transpose(1, 0, 2).reshape(C2, 8 * C1),
    )
    x_first, x_second, cot, marks, pe, dve, de = call(
        edge_kernel,
        [SMEM] + [VMEM] * 6,
        [
            shape(XMSG, 256), shape(XMSG, 256), shape(4, 96, 128), shape(128, 128),
            shape(4, 8, 112, 256), shape(4, 80, 256, dtype=F32), shape(9, 2, 96, 128),
        ],
        [pltpu.VMEM((8, 128, 256), BF16), pltpu.VMEM((2, 112, 128), BF16)],
        5 * 10**8, 10**6, flag, own, cown, y_a, y_b, w1, wd,
    )
    x_a, x_b = swaps(x_first, x_second, "gx")
    gm, qm = call(
        middle_kernel,
        [VMEM] * 9,
        [shape(9, 2, 80, 128), shape(4, 2, 64, 256)],
        [pltpu.VMEM((2, 80, 256), F32), pltpu.VMEM((9, 1, 96, 128), BF16)],
        5 * 10**9, 10**7,
        cot, marks, pe, de, w1, w3, w4, wd, wu,
    )
    return call(
        main_kernel,
        [VMEM] * 15,
        shape(32, 16, 256),
        [
            pltpu.VMEM((4, 4, 112, 256), BF16),
            pltpu.VMEM((3, 112, 128), F32),
            pltpu.VMEM((4, 80, 256), F32),
            pltpu.VMEM((9, 4, 96, 128), BF16),
            pltpu.VMEM((4, 96, 128), BF16),
            pltpu.VMEM((9, 4, 80, 128), BF16),
            pltpu.VMEM((4, 10, 64, 256), BF16),
            pltpu.VMEM((2, 512, 128), F32),
        ],
        10**10, 10**7,
        cot, marks, x_a, x_b, pe, dve, de, gm, qm, w1, w2, w3, w4, wd, wu,
    )


def solution(mesh):
    placed = (P(None, "gx", "gy"), P("gx", "gy", None), P(), P(), P(), P(None, "gx", "gy"))
    return jax.shard_map(
        on_device, mesh=mesh, in_specs=placed, out_specs=P(None, "gx", "gy"), check_vma=False
    )
```

```python
import jax
import jax.numpy as jnp
from jax import lax
from jax.experimental import pallas as pl
from jax.experimental.pallas import tpu as pltpu
from jax.sharding import PartitionSpec as P

C1 = 32
C2 = 64
LANES = 256
HALO = 4
NB = 8
WIDE = NB + 2 * HALO
YMSG = 192 + 32 + 32 + 16
XMSG = 192 + 48 + 64
F32 = jnp.float32
BF16 = jnp.bfloat16
NT = (((1,), (1,)), ((), ()))
TN = (((0,), (0,)), ((), ()))


def iota(shape, dim):
    return lax.broadcasted_iota(jnp.int32, shape, dim)


def one_hot(cond):
    return jnp.where(cond, 1.0, 0.0).astype(BF16)


def dot(a, b):
    return jnp.dot(a, b, preferred_element_type=F32)


def block_sum_matrix():
    r, l = iota((64, 256), 0), iota((64, 256), 1)
    return one_hot((r // 8 == l // 32) & (r % 8 == (l % 16) // 2))


def parity_matrix():
    r, l = iota((256, 256), 0), iota((256, 256), 1)
    return one_hot(((r // 64) % 2 == (l // 16) % 2) & ((r // 32) % 2 == l % 2))


def is_odd(axis):
    return lax.rem(lax.axis_index(axis), 2)


def constant_kernel(q_ref, parity_ref):
    q_ref[...] = block_sum_matrix()
    parity_ref[...] = parity_matrix()


def low_y(shape):
    return (iota(shape, len(shape) - 1) // 64) % 2 == 0


def pack_kernel(flag_ref, feat_ref, cot_ref, q_ref, parity_ref, own_ref, cown_ref, first_ref, second_ref, f_scr, c_scr, m_scr):
    odd = is_odd("gy")
    flag = flag_ref[0].astype(F32)
    cells = feat_ref[...].astype(F32).reshape(512, 256)
    f_scr[0] = cells[:, :128]
    f_scr[1] = cells[:, 128:]
    c_scr[:, :64] = cot_ref[...].astype(F32).reshape(512, 64) * flag
    parity = parity_ref[...]
    blocks = []
    for xb in range(NB):
        parts = []
        for a0 in range(2):
            at = pl.ds(2 * xb + a0, C1, stride=16)
            rows = jnp.concatenate([f_scr[0, at, :], f_scr[1, at, :]], axis=1).astype(BF16)
            parts += [rows] * 4
        spread = jnp.concatenate(parts, axis=0) * parity
        blocks.append(lax.dot_general(q_ref[...], spread, NT, preferred_element_type=F32))
        own_ref[xb] = blocks[xb].astype(BF16)
    for n, (inner, outer) in enumerate(((0, 24), (40, 32))):
        for j in range(4):
            rows = [blocks[2 * j + k][inner : inner + 24] for k in range(2)]
            m_scr[n, pl.ds(48 * j, 48), :] = jnp.concatenate(rows, axis=0).astype(BF16)
        rows = []
        for k in range(4):
            here, there = (blocks[k + i][outer : outer + 8] for i in (0, 4))
            there = pltpu.roll(there, 64 if n == 0 else 192, 1)
            low = low_y((8, 256))
            rows.append(jnp.where(low, here, there) if n == 0 else jnp.where(low, there, here))
        m_scr[n, pl.ds(192, 32), :] = jnp.concatenate(rows, axis=0).astype(BF16)
        m_scr[n, pl.ds(256, 16), :] = jnp.full((16, LANES), flag, F32).astype(BF16)
    eye = one_hot(iota((64, 64), 0) == iota((64, 64), 1))
    for p in range(4):
        rows = jnp.concatenate(
            [c_scr[pl.ds(2 * p + b, C2, stride=8), :] for b in range(2)], axis=0
        )[:, :64].astype(BF16)
        cells = lax.dot_general(eye, rows, NT, preferred_element_type=F32).astype(BF16)
        cown_ref[p] = cells
        at = (pl.ds(224 + 16 * (p // 2), 16), pl.ds(128 * (p % 2), 128))
        m_scr[(0, *at)] = cells[:16]
        m_scr[(1, *at)] = cells[48:]
    first_ref[...] = m_scr[odd]
    second_ref[...] = m_scr[1 - odd]


OFFSETS = {(0, 0): 0, (1, 0): 1, (0, 1): 2, (1, 1): -1}


def fine_weights(u_ref, out_ref, u_scr, v_scr, w_scr, backward):
    tile = one_hot(iota((32, 256), 0) == iota((32, 256), 1) % 32)
    u_scr[...] = dot(u_ref[...], tile).astype(BF16).reshape(27, 32, 256)
    lane = iota((32, 256), 1)
    low2 = one_hot((lane // 32) % 2 == 0), one_hot((lane // 32) % 2 == 1)
    low1 = one_hot((lane // 64) % 2 == 0), one_hot((lane // 64) % 2 == 1)

    def taps(f):
        return ((-f, 1 - f) if backward else (f, f - 1))

    def mix(load, f, masks):
        terms = [load(e) * mask for e, mask in zip(taps(f), masks) if abs(e) <= 1]
        return sum(terms[1:], terms[0])

    def body(e0, carry):
        for e1 in range(3):
            for f2 in range(-1, 3):
                v_scr[e0 * 12 + e1 * 4 + (f2 + 1)] = mix(
                    lambda e2: u_scr[e0 * 9 + e1 * 3 + e2 + 1], f2, low2
                )
        for f1 in range(-1, 3):
            for f2 in range(-1, 3):
                w_scr[e0 * 16 + (f1 + 1) * 4 + f2 + 1] = mix(
                    lambda e1: v_scr[e0 * 12 + (e1 + 1) * 4 + f2 + 1], f1, low1
                )
        return carry

    lax.fori_loop(0, 3, body, 0)
    half = jnp.zeros((32, 128), BF16)
    for my in range(2):
        for mz in range(2):
            for mx in range(2):
                for a0 in range(2):
                    for a1 in range(2):
                        for a2 in range(2):
                            f0, f1, f2 = OFFSETS[a0, mx], OFFSETS[a1, my], OFFSETS[a2, mz]
                            row = ((my * 2 + mz) * 2 + mx) * 256 + (a0 * 4 + a1 * 2 + a2) * 32
                            for b0, e0 in enumerate(taps(f0)):
                                at = (pl.ds(row, 32), pl.ds(128 * b0, 128))
                                if abs(e0) <= 1:
                                    out_ref[at] = w_scr[(e0 + 1) * 16 + (f1 + 1) * 4 + f2 + 1, :, 128 * b0 : 128 * b0 + 128]
                                else:
                                    out_ref[at] = half


def coarse_weights(u_ref, out_ref, u_scr, backward):
    if backward:
        tile = one_hot(iota((64, 128), 0) == iota((64, 128), 1) % 64)
        u_scr[...] = dot(u_ref[...], tile).astype(BF16).reshape(27, 64, 128)
    else:
        eye = one_hot(iota((64, 64), 0) == iota((64, 64), 1))
        for e in range(27):
            turned = lax.dot_general(eye, u_ref[pl.ds(64 * e, 64), :], NT, preferred_element_type=F32)
            u_scr[e] = jnp.concatenate([turned, turned], axis=1).astype(BF16)
    masks = one_hot(iota((64, 128), 1) < 64), one_hot(iota((64, 128), 1) >= 64)

    def body(t, carry):
        k = 8 - t if backward else t
        for s in range(4):
            taps = (1 - s, 2 - s) if backward else (s - 1, s - 2)
            terms = [u_scr[(e + 1) * 9 + k] * mask for e, mask in zip(taps, masks) if abs(e) <= 1]
            out_ref[pl.ds(t * 256 + s * 64, 64), :] = sum(terms[1:], terms[0])
        return carry

    lax.fori_loop(0, 9, body, 0)


def weight_kernel(
    u1_ref, u1b_ref, u2_ref, kd_ref, ku_ref,
    w1_ref, w2_ref, w3_ref, w4_ref, wd_ref, wu_ref,
    u_scr, v_scr, w_scr, uc_scr,
):
    fine_weights(u1_ref, w1_ref, u_scr, v_scr, w_scr, False)
    fine_weights(u1b_ref, w2_ref, u_scr, v_scr, w_scr, True)
    coarse_weights(u2_ref, w3_ref, uc_scr, False)
    coarse_weights(u2_ref, w4_ref, uc_scr, True)
    for b in range(2):
        place = one_hot(iota((64, 128), 0) + 64 * b == iota((64, 128), 1))
        wd_ref[pl.ds(256 * b, 256), :] = dot(kd_ref[...], place).astype(BF16)
        zero = jnp.zeros((64, 256), BF16)
        wu_ref[b, pl.ds(64 * b, 64), :] = ku_ref[...]
        wu_ref[b, pl.ds(64 * (1 - b), 64), :] = zero


def silu_parts(v):
    s = 0.5 + 0.5 * jnp.tanh(0.5 * v)
    vs = v * s
    return vs, s + vs * (1.0 - s)


def shift_z(cells, up):
    z = iota(cells.shape, 1)
    if up:
        return jnp.where(z < 7, pltpu.roll(cells, 7, 1), 0.0)
    return jnp.where(z > 0, pltpu.roll(cells, 1, 1), 0.0)


def mixed(cells, store):
    n = cells.shape[0]
    rows = (n - 2) * 8
    lane = iota(cells.shape, 2)
    zmix = jnp.where((lane // 32) % 2 == 0, shift_z(cells, True), shift_z(cells, False))
    low1 = (iota((n - 2, 8, 256), 2) // 64) % 2 == 0
    for mz, form in enumerate((cells, zmix)):
        store(mz, form[1 : n - 1].reshape(rows, 256).astype(BF16))
        store(2 + mz, jnp.where(low1, form[2:], form[: n - 2]).reshape(rows, 256).astype(BF16))


def conv_lhs(before, here, after):
    parts = []
    for m in range(4):
        parts += [here[0][m, here[1]], after[0][m, after[1], :, :128], before[0][m, before[1], :, 128:]]
    return jnp.concatenate(parts, axis=1)


def coarse_forms(cells, store):
    n = cells.shape[0]
    for dz, form in enumerate((shift_z(cells, False), cells, shift_z(cells, True))):
        for dy in range(3):
            store(dy * 3 + dz, form[dy : dy + n - 2].reshape((n - 2) * 8, 128).astype(BF16))


def storer(scr, slot):
    def store(m, value):
        scr[m, slot] = value

    return store


def pair_lhs(low, high):
    parts = []
    for t in range(9):
        parts += [low[0][t, low[1]], high[0][t, high[1]]]
    return jnp.concatenate(parts, axis=1)


def spread_block(p_scr, slot, cells):
    mixed(cells.astype(F32).reshape(16, 8, 256), storer(p_scr, slot))


def forward_pair(places, marks, w1_ref, wd_ref, dv_scr, dv_slot, d_scr, d_slot):
    lhs = jnp.concatenate([conv_lhs(*places[:3]), conv_lhs(*places[1:])], axis=0)
    pre = dot(lhs, w1_ref[...])
    hidden = []
    for b in range(2):
        value, slope = silu_parts(pre[112 * b : 112 * b + 112])
        flags = jnp.concatenate([marks(b)] * 2, axis=1)
        hidden.append((flags * value).astype(BF16))
        dv_scr[dv_slot + b] = (flags * slope)[16:96]
    down = dot(jnp.concatenate(hidden, axis=1), wd_ref[...]).astype(BF16)
    coarse_forms(down.astype(F32).reshape(14, 8, 128), storer(d_scr, d_slot))
    return down


def coarse_forward(places, cots, w3_ref, g_scr, g_first):
    lhs = jnp.concatenate([pair_lhs(*places[:2]), pair_lhs(*places[1:])], axis=0)
    pre = dot(lhs, w3_ref[...])
    for k in range(2):
        _, slope = silu_parts(pre[96 * k : 96 * k + 96])
        grad = (cots(k).astype(F32) * slope).astype(BF16)
        coarse_forms(grad.astype(F32).reshape(12, 8, 128), storer(g_scr, g_first + k))


def fine_gradient(grad, slopes, wu_ref, q_scr, slot):
    for b in range(2):
        fine = (dot(grad, wu_ref[b]) * slopes(b)).astype(BF16)
        mixed(fine.astype(F32).reshape(10, 8, 256), storer(q_scr, slot + b))


def edge_kernel(
    flag_ref, own_ref, cown_ref, ya_ref, yb_ref, w1_ref, wd_ref,
    first_ref, second_ref, cot_ref, marks_ref, p_ref, dv_ref, d_ref,
    ext_ref, down_scr,
):
    odd_y, odd_x = is_odd("gy"), is_odd("gx")

    def place(above, below):
        for xb in range(NB):
            at = 48 * (xb // 2), 24 * (xb % 2)
            inner = [ref[pl.ds(at[0], 48), :].astype(F32)[at[1] : at[1] + 24] for ref in (above, below)]
            at = 192 + 16 * ((xb % 4) // 2), 8 * (xb % 2)
            outer = [ref[pl.ds(at[0], 16), :].astype(F32)[at[1] : at[1] + 8] for ref in (above, below)]
            if xb >= 4:
                outer = [pltpu.roll(outer[0], 64, 1), pltpu.roll(outer[1], 192, 1)]
            ext_ref[xb, pl.ds(0, 8), :] = outer[0]
            ext_ref[xb, pl.ds(8, 24), :] = inner[0]
            ext_ref[xb, pl.ds(32, 64), :] = own_ref[xb].astype(F32)
            ext_ref[xb, pl.ds(96, 24), :] = inner[1]
            ext_ref[xb, pl.ds(120, 8), :] = outer[1]
        for p in range(4):
            at = (pl.ds(224 + 16 * (p // 2), 16), pl.ds(128 * (p % 2), 128))
            cot_ref[p, pl.ds(0, 16), :] = above[at]
            cot_ref[p, pl.ds(16, 64), :] = cown_ref[p]
            cot_ref[p, pl.ds(80, 16), :] = below[at]
        for k in range(2):
            marks_ref[pl.ds(16 * k, 16), :] = above[pl.ds(256, 16), pl.ds(0, 128)]
            marks_ref[pl.ds(96 + 16 * k, 16), :] = below[pl.ds(256, 16), pl.ds(0, 128)]

    marks_ref[pl.ds(32, 64), :] = jnp.full((64, 128), flag_ref[0].astype(F32), F32).astype(BF16)
    pl.when(odd_y == 1)(lambda: place(yb_ref, ya_ref))
    pl.when(odd_y == 0)(lambda: place(ya_ref, yb_ref))

    marks = marks_ref[...].astype(F32)[8:120]
    for k in range(NB):
        spread_block(p_ref, k, ext_ref[k])
    for n in range(2):
        places = [(p_ref, 4 * n + k) for k in range(4)]
        down_scr[n] = forward_pair(places, lambda b: marks, w1_ref, wd_ref, dv_ref, 2 * n, d_ref, n)

    def send(low, high):
        for ref, n, near, outer, lane in ((low, 0, 0, 1, 0), (high, 1, 7, 6, 128)):
            ref[pl.ds(0, 128), :] = ext_ref[near].astype(BF16)
            for h in range(2):
                half = pl.ds(128 * h, 128)
                ref[pl.ds(128, 64), half] = ext_ref[outer, pl.ds(64 * h, 64), pl.ds(lane, 128)].astype(BF16)
                ref[pl.ds(192, 48), half] = cot_ref[3 * n, pl.ds(48 * h, 48), :]
            ref[pl.ds(240, 64), pl.ds(0, 128)] = down_scr[n, pl.ds(0, 64), :]
            ref[pl.ds(240, 48), pl.ds(128, 128)] = down_scr[n, pl.ds(64, 48), :]
            ends = [marks_ref[pl.ds(96 * k, 16), :].astype(F32)[:8] for k in range(2)]
            own = marks_ref[pl.ds(32, 16), :].astype(F32)
            flags = jnp.where(low_y((16, 128)), jnp.concatenate(ends, axis=0), own)
            ref[pl.ds(288, 16), pl.ds(128, 128)] = flags.astype(BF16)

    pl.when(odd_x == 1)(lambda: send(second_ref, first_ref))
    pl.when(odd_x == 0)(lambda: send(first_ref, second_ref))


def middle_kernel(
    cot_ref, marks_ref, p_ref, d_ref, w1_ref, w3_ref, w4_ref, wd_ref, wu_ref,
    g_ref, q_ref,
    dv_scr, d_scr,
):
    marks = marks_ref[...].astype(F32)[8:120]
    places = [(p_ref, 2 + k) for k in range(4)]
    forward_pair(places, lambda b: marks, w1_ref, wd_ref, dv_scr, 0, d_scr, 0)
    places = [(d_ref, 0), (d_scr, 0), (d_ref, 1)]
    coarse_forward(places, lambda k: cot_ref[1 + k], w3_ref, g_ref, 0)
    grad = dot(pair_lhs((g_ref, 0), (g_ref, 1)), w4_ref[...]).astype(BF16)
    fine_gradient(grad, lambda b: dv_scr[b], wu_ref, q_ref, 0)


def main_kernel(
    cot_ref, marks_ref, xa_ref, xb_ref, pe_ref, dve_ref, de_ref, gm_ref, qm_ref,
    w1_ref, w2_ref, w3_ref, w4_ref, wd_ref, wu_ref,
    out_ref,
    p_scr, flag_scr, dv_scr, d_scr, cot_scr, g_scr, q_scr, o_scr,
):
    odd = is_odd("gx")

    def receive(left_ref, right_ref):
        sides = ((left_ref, 0, 0, 0, 1, 0, 128), (right_ref, 2, 3, 3, 2, 3, 0))
        for ref, flag_slot, cot_slot, d_slot, near, outer, lane in sides:
            flags = ref[pl.ds(288, 16), pl.ds(128, 128)].astype(F32)
            turned = pltpu.roll(flags, 64, 1)
            ends = jnp.where(low_y((16, 128)), flags, turned)
            own = jnp.where(low_y((16, 128)), turned, flags)
            flag_scr[flag_slot] = jnp.concatenate([ends[:8]] * 3 + [own] * 4 + [ends[8:]] * 3, axis=0)
            for h in range(2):
                cot_scr[cot_slot, pl.ds(48 * h, 48), :] = ref[pl.ds(192, 48), pl.ds(128 * h, 128)]
            down = [ref[pl.ds(240, 64 - 16 * h), pl.ds(128 * h, 128)] for h in range(2)]
            down = jnp.concatenate(down, axis=0).astype(F32)
            coarse_forms(down.reshape(14, 8, 128), storer(d_scr, d_slot))
            spread_block(p_scr, near, ref[pl.ds(0, 128), :])
            half = jnp.concatenate([ref[pl.ds(128, 64), pl.ds(128 * h, 128)] for h in range(2)], axis=0)
            zero = jnp.zeros((128, 128), BF16)
            spread_block(p_scr, outer, jnp.concatenate([half, zero] if lane == 0 else [zero, half], axis=1))

    pl.when(odd == 1)(lambda: receive(xb_ref, xa_ref))
    pl.when(odd == 0)(lambda: receive(xa_ref, xb_ref))
    flag_scr[1] = marks_ref[...].astype(F32)[8:120]
    cot_scr[1] = cot_ref[0]
    cot_scr[2] = cot_ref[3]
    for m in range(4):
        for k in range(2):
            q_scr[m, 4 + k] = qm_ref[m, k]

    left = [(p_scr, 0), (p_scr, 1), (pe_ref, 0), (pe_ref, 1)]
    right = [(pe_ref, 6), (pe_ref, 7), (p_scr, 2), (p_scr, 3)]
    for n, (places, regions) in enumerate(((left, (0, 1)), (right, (1, 2)))):
        forward_pair(places, lambda b: flag_scr[regions[b]], w1_ref, wd_ref, dv_scr, 2 * n, d_scr, 1 + n)

    coarse_forward([(d_scr, 0), (d_scr, 1), (de_ref, 0)], lambda k: cot_scr[k], w3_ref, g_scr, 0)
    coarse_forward([(de_ref, 1), (d_scr, 2), (d_scr, 3)], lambda k: cot_scr[2 + k], w3_ref, g_scr, 2)

    left = [(g_scr, 0), (g_scr, 1), (gm_ref, 0)]
    right = [(gm_ref, 1), (g_scr, 2), (g_scr, 3)]
    slopes = [((dv_scr, 0), (dve_ref, 0)), ((dve_ref, 2), (dv_scr, 2))]
    for n, places in enumerate((left, right)):
        lhs = jnp.concatenate([pair_lhs(*places[:2]), pair_lhs(*places[1:])], axis=0)
        grad = dot(lhs, w4_ref[...]).astype(BF16)
        for k in range(2):
            ref, slot = slopes[n][k]
            fine_gradient(grad[80 * k : 80 * k + 80], lambda b: ref[slot + b], wu_ref, q_scr, 6 * n + 2 * k)

    q = block_sum_matrix()
    parity = parity_matrix().astype(F32)
    for h in range(2):
        lhs = jnp.concatenate(
            [conv_lhs(*((q_scr, 4 * h + k + n) for n in range(3))) for k in range(4)], axis=0
        )
        grad = dot(lhs, w2_ref[...]).astype(BF16)
        for k in range(4):
            spread = lax.dot_general(grad[64 * k : 64 * k + 64], q, TN, preferred_element_type=F32) * parity
            for b in range(2):
                rows = sum(spread[128 * b + 32 * i : 128 * b + 32 * i + 32] for i in range(4))
                at = pl.ds(8 * h + 2 * k + b, C1, stride=16)
                o_scr[0, at, :] = rows[:, :128]
                o_scr[1, at, :] = rows[:, 128:]
    cells = jnp.concatenate([o_scr[0], o_scr[1]], axis=1)
    out_ref[...] = cells.reshape(32, 16, 256).astype(BF16)


VMEM = pl.BlockSpec(memory_space=pltpu.VMEM)
SMEM = pl.BlockSpec(memory_space=pltpu.SMEM)


def call(kernel, specs, outs, scratch, flops, nbytes, *args):
    return pl.pallas_call(
        kernel,
        out_shape=outs,
        in_specs=specs,
        out_specs=jax.tree.map(lambda _: VMEM, outs),
        scratch_shapes=scratch,
        compiler_params=pltpu.CompilerParams(vmem_limit_bytes=24 * 1024 * 1024),
        cost_estimate=pl.CostEstimate(flops=flops, bytes_accessed=nbytes, transcendentals=0),
    )(*args)


def shape(*dims, dtype=BF16):
    return jax.ShapeDtypeStruct(dims, dtype)


def swaps(first, second, axis):
    count = lax.axis_size(axis)

    def both_ways(start):
        edges = [(i, i + 1) for i in range(start, count - 1, 2)]
        return edges + [(j, i) for i, j in edges]

    return lax.ppermute(first, axis, both_ways(1)), lax.ppermute(second, axis, both_ways(0))


def on_device(features, brick_mask, kernel_fine, kernel_down, kernel_coarse, cotangent):
    flag = brick_mask.reshape(1)
    q, parity = call(constant_kernel, [], [shape(64, 256), shape(256, 256)], [], 4 * 10**9, 10**5)
    own, cown, y_first, y_second = call(
        pack_kernel,
        [SMEM] + [VMEM] * 4,
        [shape(8, 64, 256), shape(4, 64, 128), shape(YMSG, 256), shape(YMSG, 256)],
        [pltpu.VMEM((2, 512, 128), F32), pltpu.VMEM((512, 128), F32), pltpu.VMEM((2, YMSG, 256), BF16)],
        2 * 10**9, 10**6, flag, features, cotangent, q, parity,
    )
    y_a, y_b = swaps(y_first, y_second, "gy")
    fine = kernel_fine.reshape(27, C1, C1)
    down = kernel_down.reshape(8, C2, C1)
    w1, w2, w3, w4, wd, wu = call(
        weight_kernel,
        [VMEM] * 5,
        [shape(2048, 256), shape(2048, 256), shape(2304, 128), shape(2304, 128), shape(512, 128), shape(2, 128, 256)],
        [
            pltpu.VMEM((27, 32, 256), BF16),
            pltpu.VMEM((36, 32, 256), BF16),
            pltpu.VMEM((48, 32, 256), BF16),
            pltpu.VMEM((27, 64, 128), BF16),
        ],
        10**9, 10**7,
        fine.transpose(0, 2, 1).reshape(27 * C1, C1),
        fine.reshape(27 * C1, C1),
        kernel_coarse.reshape(27 * C2, C2),
        down.transpose(0, 2, 1).reshape(8 * C1, C2),
        down.transpose(1, 0, 2).reshape(C2, 8 * C1),
    )
    x_first, x_second, cot, marks, pe, dve, de = call(
        edge_kernel,
        [SMEM] + [VMEM] * 6,
        [
            shape(XMSG, 256), shape(XMSG, 256), shape(4, 96, 128), shape(128, 128),
            shape(4, 8, 112, 256), shape(4, 80, 256, dtype=F32), shape(9, 2, 96, 128),
        ],
        [pltpu.VMEM((8, 128, 256), F32), pltpu.VMEM((2, 112, 128), BF16)],
        5 * 10**8, 10**6, flag, own, cown, y_a, y_b, w1, wd,
    )
    x_a, x_b = swaps(x_first, x_second, "gx")
    gm, qm = call(
        middle_kernel,
        [VMEM] * 9,
        [shape(9, 2, 80, 128), shape(4, 2, 64, 256)],
        [pltpu.VMEM((2, 80, 256), F32), pltpu.VMEM((9, 1, 96, 128), BF16)],
        5 * 10**9, 10**7,
        cot, marks, pe, de, w1, w3, w4, wd, wu,
    )
    return call(
        main_kernel,
        [VMEM] * 15,
        shape(32, 16, 256),
        [
            pltpu.VMEM((4, 4, 112, 256), BF16),
            pltpu.VMEM((3, 112, 128), F32),
            pltpu.VMEM((4, 80, 256), F32),
            pltpu.VMEM((9, 4, 96, 128), BF16),
            pltpu.VMEM((4, 96, 128), BF16),
            pltpu.VMEM((9, 4, 80, 128), BF16),
            pltpu.VMEM((4, 10, 64, 256), BF16),
            pltpu.VMEM((2, 512, 128), F32),
        ],
        10**10, 10**7,
        cot, marks, x_a, x_b, pe, dve, de, gm, qm, w1, w2, w3, w4, wd, wu,
    )


def solution(mesh):
    placed = (P(None, "gx", "gy"), P("gx", "gy", None), P(), P(), P(), P(None, "gx", "gy"))
    return jax.shard_map(
        on_device, mesh=mesh, in_specs=placed, out_specs=P(None, "gx", "gy"), check_vma=False
    )
```

```python
import jax
import jax.numpy as jnp
from jax import lax
from jax.experimental import pallas as pl
from jax.experimental.pallas import tpu as pltpu
from jax.sharding import PartitionSpec as P

C1 = 32
C2 = 64
LANES = 256
HALO = 4
NB = 8
WIDE = NB + 2 * HALO
YMSG = 192 + 32 + 32 + 16
XMSG = 192 + 48 + 64
F32 = jnp.float32
BF16 = jnp.bfloat16
NT = (((1,), (1,)), ((), ()))
TN = (((0,), (0,)), ((), ()))


def iota(shape, dim):
    return lax.broadcasted_iota(jnp.int32, shape, dim)


def one_hot(cond):
    return jnp.where(cond, 1.0, 0.0).astype(BF16)


def dot(a, b):
    return jnp.dot(a, b, preferred_element_type=F32)


def block_sum_matrix():
    r, l = iota((64, 256), 0), iota((64, 256), 1)
    return one_hot((r // 8 == l // 32) & (r % 8 == (l % 16) // 2))


def parity_matrix():
    r, l = iota((256, 256), 0), iota((256, 256), 1)
    return one_hot(((r // 64) % 2 == (l // 16) % 2) & ((r // 32) % 2 == l % 2))


def is_odd(axis):
    return lax.rem(lax.axis_index(axis), 2)


def constant_kernel(q_ref, parity_ref):
    q_ref[...] = block_sum_matrix()
    parity_ref[...] = parity_matrix()


def low_y(shape):
    return (iota(shape, len(shape) - 1) // 64) % 2 == 0


def pack_kernel(flag_ref, feat_ref, cot_ref, q_ref, parity_ref, own_ref, cown_ref, first_ref, second_ref, f_scr, c_scr, m_scr):
    odd = is_odd("gy")
    flag = flag_ref[0].astype(F32)
    cells = feat_ref[...].astype(F32).reshape(512, 256)
    f_scr[0] = cells[:, :128]
    f_scr[1] = cells[:, 128:]
    c_scr[:, :64] = cot_ref[...].astype(F32).reshape(512, 64) * flag
    parity = parity_ref[...]
    blocks = []
    for xb in range(NB):
        parts = []
        for a0 in range(2):
            at = pl.ds(2 * xb + a0, C1, stride=16)
            rows = jnp.concatenate([f_scr[0, at, :], f_scr[1, at, :]], axis=1).astype(BF16)
            parts += [rows] * 4
        spread = jnp.concatenate(parts, axis=0) * parity
        blocks.append(lax.dot_general(q_ref[...], spread, NT, preferred_element_type=F32))
        own_ref[xb] = blocks[xb].astype(BF16)
    for n, (inner, outer) in enumerate(((0, 24), (40, 32))):
        for j in range(4):
            rows = [blocks[2 * j + k][inner : inner + 24] for k in range(2)]
            m_scr[n, pl.ds(48 * j, 48), :] = jnp.concatenate(rows, axis=0).astype(BF16)
        rows = []
        for k in range(4):
            here, there = (blocks[k + i][outer : outer + 8] for i in (0, 4))
            there = pltpu.roll(there, 64 if n == 0 else 192, 1)
            low = low_y((8, 256))
            rows.append(jnp.where(low, here, there) if n == 0 else jnp.where(low, there, here))
        m_scr[n, pl.ds(192, 32), :] = jnp.concatenate(rows, axis=0).astype(BF16)
        m_scr[n, pl.ds(256, 16), :] = jnp.full((16, LANES), flag, F32).astype(BF16)
    eye = one_hot(iota((64, 64), 0) == iota((64, 64), 1))
    for p in range(4):
        rows = jnp.concatenate(
            [c_scr[pl.ds(2 * p + b, C2, stride=8), :] for b in range(2)], axis=0
        )[:, :64].astype(BF16)
        cells = lax.dot_general(eye, rows, NT, preferred_element_type=F32).astype(BF16)
        cown_ref[p] = cells
        at = (pl.ds(224 + 16 * (p // 2), 16), pl.ds(128 * (p % 2), 128))
        m_scr[(0, *at)] = cells[:16]
        m_scr[(1, *at)] = cells[48:]
    first_ref[...] = m_scr[odd]
    second_ref[...] = m_scr[1 - odd]


OFFSETS = {(0, 0): 0, (1, 0): 1, (0, 1): 2, (1, 1): -1}


def fine_weights(u_ref, out_ref, u_scr, v_scr, w_scr, backward):
    tile = one_hot(iota((32, 256), 0) == iota((32, 256), 1) % 32)
    u_scr[...] = dot(u_ref[...], tile).astype(BF16).reshape(27, 32, 256)
    lane = iota((32, 256), 1)
    low2 = one_hot((lane // 32) % 2 == 0), one_hot((lane // 32) % 2 == 1)
    low1 = one_hot((lane // 64) % 2 == 0), one_hot((lane // 64) % 2 == 1)

    def taps(f):
        return ((-f, 1 - f) if backward else (f, f - 1))

    def mix(load, f, masks):
        terms = [load(e) * mask for e, mask in zip(taps(f), masks) if abs(e) <= 1]
        return sum(terms[1:], terms[0])

    def body(e0, carry):
        for e1 in range(3):
            for f2 in range(-1, 3):
                v_scr[e0 * 12 + e1 * 4 + (f2 + 1)] = mix(
                    lambda e2: u_scr[e0 * 9 + e1 * 3 + e2 + 1], f2, low2
                )
        for f1 in range(-1, 3):
            for f2 in range(-1, 3):
                w_scr[e0 * 16 + (f1 + 1) * 4 + f2 + 1] = mix(
                    lambda e1: v_scr[e0 * 12 + (e1 + 1) * 4 + f2 + 1], f1, low1
                )
        return carry

    lax.fori_loop(0, 3, body, 0)
    half = jnp.zeros((32, 128), BF16)
    for my in range(2):
        for mz in range(2):
            for mx in range(2):
                for a0 in range(2):
                    for a1 in range(2):
                        for a2 in range(2):
                            f0, f1, f2 = OFFSETS[a0, mx], OFFSETS[a1, my], OFFSETS[a2, mz]
                            row = ((my * 2 + mz) * 2 + mx) * 256 + (a0 * 4 + a1 * 2 + a2) * 32
                            for b0, e0 in enumerate(taps(f0)):
                                at = (pl.ds(row, 32), pl.ds(128 * b0, 128))
                                if abs(e0) <= 1:
                                    out_ref[at] = w_scr[(e0 + 1) * 16 + (f1 + 1) * 4 + f2 + 1, :, 128 * b0 : 128 * b0 + 128]
                                else:
                                    out_ref[at] = half


def coarse_weights(u_ref, out_ref, u_scr, backward):
    if backward:
        tile = one_hot(iota((64, 128), 0) == iota((64, 128), 1) % 64)
        u_scr[...] = dot(u_ref[...], tile).astype(BF16).reshape(27, 64, 128)
    else:
        eye = one_hot(iota((64, 64), 0) == iota((64, 64), 1))
        for e in range(27):
            turned = lax.dot_general(eye, u_ref[pl.ds(64 * e, 64), :], NT, preferred_element_type=F32)
            u_scr[e] = jnp.concatenate([turned, turned], axis=1).astype(BF16)
    masks = one_hot(iota((64, 128), 1) < 64), one_hot(iota((64, 128), 1) >= 64)

    def body(t, carry):
        k = 8 - t if backward else t
        for s in range(4):
            taps = (1 - s, 2 - s) if backward else (s - 1, s - 2)
            terms = [u_scr[(e + 1) * 9 + k] * mask for e, mask in zip(taps, masks) if abs(e) <= 1]
            out_ref[pl.ds(t * 256 + s * 64, 64), :] = sum(terms[1:], terms[0])
        return carry

    lax.fori_loop(0, 9, body, 0)


def weight_kernel(
    u1_ref, u1b_ref, u2_ref, kd_ref, ku_ref,
    w1_ref, w2_ref, w3_ref, w4_ref, wd_ref, wu_ref,
    u_scr, v_scr, w_scr, uc_scr,
):
    fine_weights(u1_ref, w1_ref, u_scr, v_scr, w_scr, False)
    fine_weights(u1b_ref, w2_ref, u_scr, v_scr, w_scr, True)
    coarse_weights(u2_ref, w3_ref, uc_scr, False)
    coarse_weights(u2_ref, w4_ref, uc_scr, True)
    for b in range(2):
        place = one_hot(iota((64, 128), 0) + 64 * b == iota((64, 128), 1))
        wd_ref[pl.ds(256 * b, 256), :] = dot(kd_ref[...], place).astype(BF16)
        zero = jnp.zeros((64, 256), BF16)
        wu_ref[b, pl.ds(64 * b, 64), :] = ku_ref[...]
        wu_ref[b, pl.ds(64 * (1 - b), 64), :] = zero


def silu_parts(v):
    s = 0.5 + 0.5 * jnp.tanh(0.5 * v)
    vs = v * s
    return vs, s + vs * (1.0 - s)


def shift_z(cells, up):
    z = iota(cells.shape, 1)
    if up:
        return jnp.where(z < 7, pltpu.roll(cells, 7, 1), 0.0)
    return jnp.where(z > 0, pltpu.roll(cells, 1, 1), 0.0)


def mixed(cells, store):
    n = cells.shape[0]
    rows = (n - 2) * 8
    lane = iota(cells.shape, 2)
    zmix = jnp.where((lane // 32) % 2 == 0, shift_z(cells, True), shift_z(cells, False))
    low1 = (iota((n - 2, 8, 256), 2) // 64) % 2 == 0
    for mz, form in enumerate((cells, zmix)):
        store(mz, form[1 : n - 1].reshape(rows, 256).astype(BF16))
        store(2 + mz, jnp.where(low1, form[2:], form[: n - 2]).reshape(rows, 256).astype(BF16))


def conv_lhs(before, here, after):
    parts = []
    for m in range(4):
        parts += [here[0][m, here[1]], after[0][m, after[1], :, :128], before[0][m, before[1], :, 128:]]
    return jnp.concatenate(parts, axis=1)


def coarse_forms(cells, store):
    n = cells.shape[0]
    for dz, form in enumerate((shift_z(cells, False), cells, shift_z(cells, True))):
        for dy in range(3):
            store(dy * 3 + dz, form[dy : dy + n - 2].reshape((n - 2) * 8, 128).astype(BF16))


def storer(scr, slot):
    def store(m, value):
        scr[m, slot] = value

    return store


def pair_lhs(low, high):
    parts = []
    for t in range(9):
        parts += [low[0][t, low[1]], high[0][t, high[1]]]
    return jnp.concatenate(parts, axis=1)


def spread_block(p_scr, slot, cells):
    mixed(cells.astype(F32).reshape(16, 8, 256), storer(p_scr, slot))


def forward_pair(places, marks, w1_ref, wd_ref, dv_scr, dv_slot, d_scr, d_slot):
    lhs = jnp.concatenate([conv_lhs(*places[:3]), conv_lhs(*places[1:])], axis=0)
    pre = dot(lhs, w1_ref[...])
    hidden = []
    for b in range(2):
        value, slope = silu_parts(pre[112 * b : 112 * b + 112])
        flags = jnp.concatenate([marks(b)] * 2, axis=1)
        hidden.append((flags * value).astype(BF16))
        dv_scr[dv_slot + b] = (flags * slope)[16:96]
    down = dot(jnp.concatenate(hidden, axis=1), wd_ref[...]).astype(BF16)
    coarse_forms(down.astype(F32).reshape(14, 8, 128), storer(d_scr, d_slot))
    return down


def coarse_forward(places, cots, w3_ref, g_scr, g_first):
    lhs = jnp.concatenate([pair_lhs(*places[:2]), pair_lhs(*places[1:])], axis=0)
    pre = dot(lhs, w3_ref[...])
    for k in range(2):
        _, slope = silu_parts(pre[96 * k : 96 * k + 96])
        grad = (cots(k).astype(F32) * slope).astype(BF16)
        coarse_forms(grad.astype(F32).reshape(12, 8, 128), storer(g_scr, g_first + k))


def fine_gradient(grad, slopes, wu_ref, q_scr, slot):
    for b in range(2):
        fine = (dot(grad, wu_ref[b]) * slopes(b)).astype(BF16)
        mixed(fine.astype(F32).reshape(10, 8, 256), storer(q_scr, slot + b))


def edge_kernel(
    flag_ref, own_ref, cown_ref, ya_ref, yb_ref, w1_ref, wd_ref,
    first_ref, second_ref, cot_ref, marks_ref, p_ref, dv_ref, d_ref,
    ext_ref, down_scr,
):
    odd_y, odd_x = is_odd("gy"), is_odd("gx")

    def place(above, below):
        for xb in range(NB):
            at = 48 * (xb // 2), 24 * (xb % 2)
            inner = [ref[pl.ds(at[0], 48), :].astype(F32)[at[1] : at[1] + 24] for ref in (above, below)]
            at = 192 + 16 * ((xb % 4) // 2), 8 * (xb % 2)
            outer = [ref[pl.ds(at[0], 16), :].astype(F32)[at[1] : at[1] + 8] for ref in (above, below)]
            if xb >= 4:
                outer = [pltpu.roll(outer[0], 64, 1), pltpu.roll(outer[1], 192, 1)]
            ext_ref[xb, pl.ds(0, 8), :] = outer[0]
            ext_ref[xb, pl.ds(8, 24), :] = inner[0]
            ext_ref[xb, pl.ds(32, 64), :] = own_ref[xb].astype(F32)
            ext_ref[xb, pl.ds(96, 24), :] = inner[1]
            ext_ref[xb, pl.ds(120, 8), :] = outer[1]
        for p in range(4):
            at = (pl.ds(224 + 16 * (p // 2), 16), pl.ds(128 * (p % 2), 128))
            cot_ref[p, pl.ds(0, 16), :] = above[at]
            cot_ref[p, pl.ds(16, 64), :] = cown_ref[p]
            cot_ref[p, pl.ds(80, 16), :] = below[at]
        for k in range(2):
            marks_ref[pl.ds(16 * k, 16), :] = above[pl.ds(256, 16), pl.ds(0, 128)]
            marks_ref[pl.ds(96 + 16 * k, 16), :] = below[pl.ds(256, 16), pl.ds(0, 128)]

    marks_ref[pl.ds(32, 64), :] = jnp.full((64, 128), flag_ref[0].astype(F32), F32).astype(BF16)
    pl.when(odd_y == 1)(lambda: place(yb_ref, ya_ref))
    pl.when(odd_y == 0)(lambda: place(ya_ref, yb_ref))

    marks = marks_ref[...].astype(F32)[8:120]
    for k in range(NB):
        spread_block(p_ref, k, ext_ref[k])
    for n in range(2):
        places = [(p_ref, 4 * n + k) for k in range(4)]
        down_scr[n] = forward_pair(places, lambda b: marks, w1_ref, wd_ref, dv_ref, 2 * n, d_ref, n)

    def send(low, high):
        for ref, n, near, outer, lane in ((low, 0, 0, 1, 0), (high, 1, 7, 6, 128)):
            ref[pl.ds(0, 128), :] = ext_ref[near].astype(BF16)
            for h in range(2):
                half = pl.ds(128 * h, 128)
                ref[pl.ds(128, 64), half] = ext_ref[outer, pl.ds(64 * h, 64), pl.ds(lane, 128)].astype(BF16)
                ref[pl.ds(192, 48), half] = cot_ref[3 * n, pl.ds(48 * h, 48), :]
            ref[pl.ds(240, 64), pl.ds(0, 128)] = down_scr[n, pl.ds(0, 64), :]
            ref[pl.ds(240, 48), pl.ds(128, 128)] = down_scr[n, pl.ds(64, 48), :]
            ends = [marks_ref[pl.ds(96 * k, 16), :].astype(F32)[:8] for k in range(2)]
            own = marks_ref[pl.ds(32, 16), :].astype(F32)
            flags = jnp.where(low_y((16, 128)), jnp.concatenate(ends, axis=0), own)
            ref[pl.ds(288, 16), pl.ds(128, 128)] = flags.astype(BF16)

    pl.when(odd_x == 1)(lambda: send(second_ref, first_ref))
    pl.when(odd_x == 0)(lambda: send(first_ref, second_ref))


def middle_kernel(
    cot_ref, marks_ref, p_ref, d_ref, w1_ref, w3_ref, w4_ref, wd_ref, wu_ref,
    g_ref, q_ref,
    dv_scr, d_scr,
):
    marks = marks_ref[...].astype(F32)[8:120]
    places = [(p_ref, 2 + k) for k in range(4)]
    forward_pair(places, lambda b: marks, w1_ref, wd_ref, dv_scr, 0, d_scr, 0)
    places = [(d_ref, 0), (d_scr, 0), (d_ref, 1)]
    coarse_forward(places, lambda k: cot_ref[1 + k], w3_ref, g_ref, 0)
    grad = dot(pair_lhs((g_ref, 0), (g_ref, 1)), w4_ref[...]).astype(BF16)
    fine_gradient(grad, lambda b: dv_scr[b], wu_ref, q_ref, 0)


def side_steps(
    side, msg_ref, cot_ref, marks_ref, pe_ref, dve_ref, de_ref, gm_ref, qm_ref, q_ref, parity_ref,
    w1_ref, w2_ref, w3_ref, w4_ref, wd_ref, wu_ref,
    store_out, scratch,
):
    p_scr, flag_scr, dv_scr, d_scr, cot_scr, g_scr, q_scr = scratch
    other = 1 - side
    right = side.astype(F32)

    spread_block(p_scr, 1 + side, msg_ref[pl.ds(0, 128), :])
    half = [msg_ref[pl.ds(128, 64), pl.ds(128 * h, 128)] for h in range(2)]
    half = jnp.concatenate(half, axis=0).astype(F32)
    spread_block(p_scr, 3 * side, jnp.concatenate([half * right, half * (1.0 - right)], axis=1))
    for k in range(2):
        for m in range(4):
            p_scr[m, 2 * other + k] = pe_ref[m, 6 * side + k]
        dv_scr[2 * other + k] = dve_ref[2 * side + k]
    flags = msg_ref[pl.ds(288, 16), pl.ds(128, 128)].astype(F32)
    turned = pltpu.roll(flags, 64, 1)
    ends = jnp.where(low_y((16, 128)), flags, turned)
    own = jnp.where(low_y((16, 128)), turned, flags)
    flag_scr[side] = jnp.concatenate([ends[:8]] * 3 + [own] * 4 + [ends[8:]] * 3, axis=0)
    flag_scr[other] = marks_ref[...].astype(F32)[8:120]
    for h in range(2):
        cot_scr[side, pl.ds(48 * h, 48), :] = msg_ref[pl.ds(192, 48), pl.ds(128 * h, 128)]
    cot_scr[other] = cot_ref[3 * side]
    down = [msg_ref[pl.ds(240, 64 - 16 * h), pl.ds(128 * h, 128)] for h in range(2)]
    down = jnp.concatenate(down, axis=0).astype(F32)
    coarse_forms(down.reshape(14, 8, 128), storer(d_scr, 2 * side))
    for t in range(9):
        d_scr[t, 2 * other] = de_ref[t, side]
        g_scr[t, 2 * other] = gm_ref[t, side]
    for m in range(4):
        for k in range(2):
            q_scr[m, 4 * other + k] = qm_ref[m, k]

    places = [(p_scr, k) for k in range(4)]
    forward_pair(places, lambda b: flag_scr[b], w1_ref, wd_ref, dv_scr, 2 * side, d_scr, 1)
    coarse_forward([(d_scr, k) for k in range(3)], lambda k: cot_scr[k], w3_ref, g_scr, side)
    lhs = jnp.concatenate([pair_lhs((g_scr, k), (g_scr, k + 1)) for k in range(2)], axis=0)
    grad = dot(lhs, w4_ref[...]).astype(BF16)
    for k in range(2):
        fine_gradient(grad[80 * k : 80 * k + 80], lambda b: dv_scr[2 * k + b], wu_ref, q_scr, 2 * side + 2 * k)
    lhs = jnp.concatenate([conv_lhs(*((q_scr, k + n) for n in range(3))) for k in range(4)], axis=0)
    grad = dot(lhs, w2_ref[...]).astype(BF16)
    parity = parity_ref[...].astype(F32)
    for k in range(4):
        spread = lax.dot_general(grad[64 * k : 64 * k + 64], q_ref[...], TN, preferred_element_type=F32) * parity
        for b in range(2):
            rows = sum(spread[128 * b + 32 * i : 128 * b + 32 * i + 32] for i in range(4))
            store_out(2 * k + b, rows)


def near_kernel(msg_ref, *refs):
    inputs, out_ref, scratch = refs[:15], refs[15], refs[16:]

    def store_out(x, rows):
        for h in range(2):
            out_ref[h, pl.ds(x, C1, stride=8), :] = rows[:, 128 * h : 128 * h + 128]

    side_steps(1 - is_odd("gx"), msg_ref, *inputs, store_out, scratch)


def far_kernel(msg_ref, near_ref, *refs):
    inputs, out_ref, scratch, o_scr = refs[:15], refs[15], refs[16:-1], refs[-1]
    side = is_odd("gx")
    o_scr[1 - side] = near_ref[...]

    def store_out(x, rows):
        for h in range(2):
            o_scr[side, h, pl.ds(x, C1, stride=8), :] = rows[:, 128 * h : 128 * h + 128]

    side_steps(side, msg_ref, *inputs, store_out, scratch)
    halves = [jnp.concatenate([o_scr[n, h].reshape(32, 8, 128) for h in range(2)], axis=2) for n in range(2)]
    out_ref[...] = jnp.concatenate(halves, axis=1).astype(BF16)


SIDE_SCRATCH = [
    pltpu.VMEM((4, 4, 112, 256), BF16),
    pltpu.VMEM((2, 112, 128), F32),
    pltpu.VMEM((4, 80, 256), F32),
    pltpu.VMEM((9, 3, 96, 128), BF16),
    pltpu.VMEM((2, 96, 128), BF16),
    pltpu.VMEM((9, 3, 80, 128), BF16),
    pltpu.VMEM((4, 6, 64, 256), BF16),
]
VMEM = pl.BlockSpec(memory_space=pltpu.VMEM)
SMEM = pl.BlockSpec(memory_space=pltpu.SMEM)


def call(kernel, specs, outs, scratch, flops, nbytes, *args):
    return pl.pallas_call(
        kernel,
        out_shape=outs,
        in_specs=specs,
        out_specs=jax.tree.map(lambda _: VMEM, outs),
        scratch_shapes=scratch,
        compiler_params=pltpu.CompilerParams(vmem_limit_bytes=24 * 1024 * 1024),
        cost_estimate=pl.CostEstimate(flops=flops, bytes_accessed=nbytes, transcendentals=0),
    )(*args)


def shape(*dims, dtype=BF16):
    return jax.ShapeDtypeStruct(dims, dtype)


def swaps(first, second, axis):
    count = lax.axis_size(axis)

    def both_ways(start):
        edges = [(i, i + 1) for i in range(start, count - 1, 2)]
        return edges + [(j, i) for i, j in edges]

    return lax.ppermute(first, axis, both_ways(1)), lax.ppermute(second, axis, both_ways(0))


def on_device(features, brick_mask, kernel_fine, kernel_down, kernel_coarse, cotangent):
    flag = brick_mask.reshape(1)
    q, parity = call(constant_kernel, [], [shape(64, 256), shape(256, 256)], [], 4 * 10**9, 10**5)
    own, cown, y_first, y_second = call(
        pack_kernel,
        [SMEM] + [VMEM] * 4,
        [shape(8, 64, 256), shape(4, 64, 128), shape(YMSG, 256), shape(YMSG, 256)],
        [pltpu.VMEM((2, 512, 128), F32), pltpu.VMEM((512, 128), F32), pltpu.VMEM((2, YMSG, 256), BF16)],
        2 * 10**9, 10**6, flag, features, cotangent, q, parity,
    )
    y_a, y_b = swaps(y_first, y_second, "gy")
    fine = kernel_fine.reshape(27, C1, C1)
    down = kernel_down.reshape(8, C2, C1)
    w1, w2, w3, w4, wd, wu = call(
        weight_kernel,
        [VMEM] * 5,
        [shape(2048, 256), shape(2048, 256), shape(2304, 128), shape(2304, 128), shape(512, 128), shape(2, 128, 256)],
        [
            pltpu.VMEM((27, 32, 256), BF16),
            pltpu.VMEM((36, 32, 256), BF16),
            pltpu.VMEM((48, 32, 256), BF16),
            pltpu.VMEM((27, 64, 128), BF16),
        ],
        10**9, 10**7,
        fine.transpose(0, 2, 1).reshape(27 * C1, C1),
        fine.reshape(27 * C1, C1),
        kernel_coarse.reshape(27 * C2, C2),
        down.transpose(0, 2, 1).reshape(8 * C1, C2),
        down.transpose(1, 0, 2).reshape(C2, 8 * C1),
    )
    x_first, x_second, cot, marks, pe, dve, de = call(
        edge_kernel,
        [SMEM] + [VMEM] * 6,
        [
            shape(XMSG, 256), shape(XMSG, 256), shape(4, 96, 128), shape(128, 128),
            shape(4, 8, 112, 256), shape(4, 80, 256, dtype=F32), shape(9, 2, 96, 128),
        ],
        [pltpu.VMEM((8, 128, 256), F32), pltpu.VMEM((2, 112, 128), BF16)],
        5 * 10**8, 10**6, flag, own, cown, y_a, y_b, w1, wd,
    )
    x_a, x_b = swaps(x_first, x_second, "gx")
    gm, qm = call(
        middle_kernel,
        [VMEM] * 9,
        [shape(9, 2, 80, 128), shape(4, 2, 64, 256)],
        [pltpu.VMEM((2, 80, 256), F32), pltpu.VMEM((9, 1, 96, 128), BF16)],
        2 * 10**10, 10**7,
        cot, marks, pe, de, w1, w3, w4, wd, wu,
    )
    shared = (cot, marks, pe, dve, de, gm, qm, q, parity, w1, w2, w3, w4, wd, wu)
    near = call(
        near_kernel,
        [VMEM] * 16,
        shape(2, 256, 128, dtype=F32),
        SIDE_SCRATCH,
        2 * 10**10, 10**7, x_b, *shared,
    )
    return call(
        far_kernel,
        [VMEM] * 17,
        shape(32, 16, 256),
        SIDE_SCRATCH + [pltpu.VMEM((2, 2, 256, 128), F32)],
        10**10, 10**7, x_a, near, *shared,
    )


def solution(mesh):
    placed = (P(None, "gx", "gy"), P("gx", "gy", None), P(), P(), P(), P(None, "gx", "gy"))
    return jax.shard_map(
        on_device, mesh=mesh, in_specs=placed, out_specs=P(None, "gx", "gy"), check_vma=False
    )
```

```python
import jax
import jax.numpy as jnp
from jax import lax
from jax.experimental import pallas as pl
from jax.experimental.pallas import tpu as pltpu
from jax.sharding import PartitionSpec as P

C1 = 32
C2 = 64
LANES = 256
HALO = 4
NB = 8
WIDE = NB + 2 * HALO
YMSG = 192 + 32 + 32 + 16
XMSG = 192 + 48 + 64
F32 = jnp.float32
BF16 = jnp.bfloat16
NT = (((1,), (1,)), ((), ()))
TN = (((0,), (0,)), ((), ()))


def iota(shape, dim):
    return lax.broadcasted_iota(jnp.int32, shape, dim)


def one_hot(cond):
    return jnp.where(cond, 1.0, 0.0).astype(BF16)


def dot(a, b):
    return jnp.dot(a, b, preferred_element_type=F32)


def block_sum_matrix():
    r, l = iota((64, 256), 0), iota((64, 256), 1)
    return one_hot((r // 8 == l // 32) & (r % 8 == (l % 16) // 2))


def parity_matrix():
    r, l = iota((256, 256), 0), iota((256, 256), 1)
    return one_hot(((r // 64) % 2 == (l // 16) % 2) & ((r // 32) % 2 == l % 2))


def is_odd(axis):
    return lax.rem(lax.axis_index(axis), 2)


def constant_kernel(q_ref, parity_ref):
    q_ref[...] = block_sum_matrix()
    parity_ref[...] = parity_matrix()


def low_y(shape):
    return (iota(shape, len(shape) - 1) // 64) % 2 == 0


def pack_kernel(flag_ref, feat_ref, cot_ref, q_ref, parity_ref, own_ref, cown_ref, first_ref, second_ref, f_scr, c_scr, m_scr):
    odd = is_odd("gy")
    flag = flag_ref[0].astype(F32)
    cells = feat_ref[...].astype(F32).reshape(512, 256)
    f_scr[0] = cells[:, :128]
    f_scr[1] = cells[:, 128:]
    c_scr[:, :64] = cot_ref[...].astype(F32).reshape(512, 64) * flag
    parity = parity_ref[...]
    blocks = []
    for xb in range(NB):
        parts = []
        for a0 in range(2):
            at = pl.ds(2 * xb + a0, C1, stride=16)
            rows = jnp.concatenate([f_scr[0, at, :], f_scr[1, at, :]], axis=1).astype(BF16)
            parts += [rows] * 4
        spread = jnp.concatenate(parts, axis=0) * parity
        blocks.append(lax.dot_general(q_ref[...], spread, NT, preferred_element_type=F32))
        own_ref[xb] = blocks[xb].astype(BF16)
    for n, (inner, outer) in enumerate(((0, 24), (40, 32))):
        for j in range(4):
            rows = [blocks[2 * j + k][inner : inner + 24] for k in range(2)]
            m_scr[n, pl.ds(48 * j, 48), :] = jnp.concatenate(rows, axis=0).astype(BF16)
        rows = []
        for k in range(4):
            here, there = (blocks[k + i][outer : outer + 8] for i in (0, 4))
            there = pltpu.roll(there, 64 if n == 0 else 192, 1)
            low = low_y((8, 256))
            rows.append(jnp.where(low, here, there) if n == 0 else jnp.where(low, there, here))
        m_scr[n, pl.ds(192, 32), :] = jnp.concatenate(rows, axis=0).astype(BF16)
        m_scr[n, pl.ds(256, 16), :] = jnp.full((16, LANES), flag, F32).astype(BF16)
    eye = one_hot(iota((64, 64), 0) == iota((64, 64), 1))
    for p in range(4):
        rows = jnp.concatenate(
            [c_scr[pl.ds(2 * p + b, C2, stride=8), :] for b in range(2)], axis=0
        )[:, :64].astype(BF16)
        cells = lax.dot_general(eye, rows, NT, preferred_element_type=F32).astype(BF16)
        cown_ref[p] = cells
        at = (pl.ds(224 + 16 * (p // 2), 16), pl.ds(128 * (p % 2), 128))
        m_scr[(0, *at)] = cells[:16]
        m_scr[(1, *at)] = cells[48:]
    first_ref[...] = m_scr[odd]
    second_ref[...] = m_scr[1 - odd]


OFFSETS = {(0, 0): 0, (1, 0): 1, (0, 1): 2, (1, 1): -1}


def fine_weights(u_ref, out_ref, u_scr, v_scr, w_scr, backward):
    tile = one_hot(iota((32, 256), 0) == iota((32, 256), 1) % 32)
    taps_in = u_ref[...]
    if not backward:
        eye = one_hot(iota((32, 32), 0) == iota((32, 32), 1))
        turned = lax.dot_general(eye, taps_in, NT, preferred_element_type=F32)
        taps_in = jnp.concatenate([turned[:, 32 * e : 32 * e + 32] for e in range(27)], axis=0).astype(BF16)
    u_scr[...] = dot(taps_in, tile).astype(BF16).reshape(27, 32, 256)
    lane = iota((32, 256), 1)
    low2 = one_hot((lane // 32) % 2 == 0), one_hot((lane // 32) % 2 == 1)
    low1 = one_hot((lane // 64) % 2 == 0), one_hot((lane // 64) % 2 == 1)

    def taps(f):
        return ((-f, 1 - f) if backward else (f, f - 1))

    def mix(load, f, masks):
        terms = [load(e) * mask for e, mask in zip(taps(f), masks) if abs(e) <= 1]
        return sum(terms[1:], terms[0])

    def body(e0, carry):
        for e1 in range(3):
            for f2 in range(-1, 3):
                v_scr[e0 * 12 + e1 * 4 + (f2 + 1)] = mix(
                    lambda e2: u_scr[e0 * 9 + e1 * 3 + e2 + 1], f2, low2
                )
        for f1 in range(-1, 3):
            for f2 in range(-1, 3):
                w_scr[e0 * 16 + (f1 + 1) * 4 + f2 + 1] = mix(
                    lambda e1: v_scr[e0 * 12 + (e1 + 1) * 4 + f2 + 1], f1, low1
                )
        return carry

    lax.fori_loop(0, 3, body, 0)
    half = jnp.zeros((32, 128), BF16)
    for my in range(2):
        for mz in range(2):
            for mx in range(2):
                for a0 in range(2):
                    for a1 in range(2):
                        for a2 in range(2):
                            f0, f1, f2 = OFFSETS[a0, mx], OFFSETS[a1, my], OFFSETS[a2, mz]
                            row = ((my * 2 + mz) * 2 + mx) * 256 + (a0 * 4 + a1 * 2 + a2) * 32
                            for b0, e0 in enumerate(taps(f0)):
                                at = (pl.ds(row, 32), pl.ds(128 * b0, 128))
                                if abs(e0) <= 1:
                                    out_ref[at] = w_scr[(e0 + 1) * 16 + (f1 + 1) * 4 + f2 + 1, :, 128 * b0 : 128 * b0 + 128]
                                else:
                                    out_ref[at] = half


def coarse_weights(u_ref, out_ref, u_scr, backward):
    if backward:
        tile = one_hot(iota((64, 128), 0) == iota((64, 128), 1) % 64)
        u_scr[...] = dot(u_ref[...], tile).astype(BF16).reshape(27, 64, 128)
    else:
        eye = one_hot(iota((64, 64), 0) == iota((64, 64), 1))
        for e in range(27):
            turned = lax.dot_general(eye, u_ref[pl.ds(64 * e, 64), :], NT, preferred_element_type=F32)
            u_scr[e] = jnp.concatenate([turned, turned], axis=1).astype(BF16)
    masks = one_hot(iota((64, 128), 1) < 64), one_hot(iota((64, 128), 1) >= 64)

    def body(t, carry):
        k = 8 - t if backward else t
        for s in range(4):
            taps = (1 - s, 2 - s) if backward else (s - 1, s - 2)
            terms = [u_scr[(e + 1) * 9 + k] * mask for e, mask in zip(taps, masks) if abs(e) <= 1]
            out_ref[pl.ds(t * 256 + s * 64, 64), :] = sum(terms[1:], terms[0])
        return carry

    lax.fori_loop(0, 9, body, 0)


def weight_kernel(
    u1_ref, u2_ref, ud_ref,
    w1_ref, w2_ref, w3_ref, w4_ref, wd_ref, wu_ref,
    u_scr, v_scr, w_scr, uc_scr,
):
    fine_weights(u1_ref, w1_ref, u_scr, v_scr, w_scr, False)
    fine_weights(u1_ref, w2_ref, u_scr, v_scr, w_scr, True)
    coarse_weights(u2_ref, w3_ref, uc_scr, False)
    coarse_weights(u2_ref, w4_ref, uc_scr, True)
    lane = iota((32, 256), 1)
    up = sum(
        dot(ud_ref[pl.ds(64 * a, 64), :], one_hot(iota((32, 256), 0) + 32 * a == lane)) for a in range(8)
    ).astype(BF16)
    for b in range(2):
        place = one_hot(iota((64, 128), 0) + 64 * b == iota((64, 128), 1))
        turned = lax.dot_general(up, place, TN, preferred_element_type=F32)
        wd_ref[pl.ds(256 * b, 256), :] = turned.astype(BF16)
        wu_ref[b, pl.ds(64 * b, 64), :] = up
        wu_ref[b, pl.ds(64 * (1 - b), 64), :] = jnp.zeros((64, 256), BF16)


def silu_parts(v):
    s = 0.5 + 0.5 * jnp.tanh(0.5 * v)
    vs = v * s
    return vs, s + vs * (1.0 - s)


def shift_z(cells, up):
    z = iota(cells.shape, 1)
    if up:
        return jnp.where(z < 7, pltpu.roll(cells, 7, 1), 0.0)
    return jnp.where(z > 0, pltpu.roll(cells, 1, 1), 0.0)


def mixed(cells, store):
    n = cells.shape[0]
    rows = (n - 2) * 8
    lane = iota(cells.shape, 2)
    zmix = jnp.where((lane // 32) % 2 == 0, shift_z(cells, True), shift_z(cells, False))
    low1 = (iota((n - 2, 8, 256), 2) // 64) % 2 == 0
    for mz, form in enumerate((cells, zmix)):
        store(mz, form[1 : n - 1].reshape(rows, 256).astype(BF16))
        store(2 + mz, jnp.where(low1, form[2:], form[: n - 2]).reshape(rows, 256).astype(BF16))


def conv_lhs(before, here, after):
    parts = []
    for m in range(4):
        parts += [here[0][m, here[1]], after[0][m, after[1], :, :128], before[0][m, before[1], :, 128:]]
    return jnp.concatenate(parts, axis=1)


def coarse_forms(cells, store):
    n = cells.shape[0]
    for dz, form in enumerate((shift_z(cells, False), cells, shift_z(cells, True))):
        for dy in range(3):
            store(dy * 3 + dz, form[dy : dy + n - 2].reshape((n - 2) * 8, 128).astype(BF16))


def storer(scr, slot):
    def store(m, value):
        scr[m, slot] = value

    return store


def pair_lhs(low, high):
    parts = []
    for t in range(9):
        parts += [low[0][t, low[1]], high[0][t, high[1]]]
    return jnp.concatenate(parts, axis=1)


def spread_block(p_scr, slot, cells):
    mixed(cells.astype(F32).reshape(16, 8, 256), storer(p_scr, slot))


def forward_pair(places, marks, w1_ref, wd_ref, dv_scr, dv_slot, d_scr, d_slot):
    lhs = jnp.concatenate([conv_lhs(*places[:3]), conv_lhs(*places[1:])], axis=0)
    pre = dot(lhs, w1_ref[...])
    hidden = []
    for b in range(2):
        value, slope = silu_parts(pre[112 * b : 112 * b + 112])
        flags = jnp.concatenate([marks(b)] * 2, axis=1)
        hidden.append((flags * value).astype(BF16))
        dv_scr[dv_slot + b] = (flags * slope)[16:96]
    down = dot(jnp.concatenate(hidden, axis=1), wd_ref[...]).astype(BF16)
    coarse_forms(down.astype(F32).reshape(14, 8, 128), storer(d_scr, d_slot))
    return down


def coarse_forward(places, cots, w3_ref, g_scr, g_first):
    lhs = jnp.concatenate([pair_lhs(*places[:2]), pair_lhs(*places[1:])], axis=0)
    pre = dot(lhs, w3_ref[...])
    for k in range(2):
        _, slope = silu_parts(pre[96 * k : 96 * k + 96])
        grad = (cots(k).astype(F32) * slope).astype(BF16)
        coarse_forms(grad.astype(F32).reshape(12, 8, 128), storer(g_scr, g_first + k))


def fine_gradient(grad, slopes, wu_ref, q_scr, slot):
    for b in range(2):
        fine = (dot(grad, wu_ref[b]) * slopes(b)).astype(BF16)
        mixed(fine.astype(F32).reshape(10, 8, 256), storer(q_scr, slot + b))


def edge_kernel(
    flag_ref, own_ref, cown_ref, ya_ref, yb_ref, w1_ref, wd_ref,
    first_ref, second_ref, cot_ref, marks_ref, p_ref, dv_ref, d_ref,
    ext_ref, down_scr,
):
    odd_y, odd_x = is_odd("gy"), is_odd("gx")

    def place(above, below):
        for xb in range(NB):
            at = 48 * (xb // 2), 24 * (xb % 2)
            inner = [ref[pl.ds(at[0], 48), :].astype(F32)[at[1] : at[1] + 24] for ref in (above, below)]
            at = 192 + 16 * ((xb % 4) // 2), 8 * (xb % 2)
            outer = [ref[pl.ds(at[0], 16), :].astype(F32)[at[1] : at[1] + 8] for ref in (above, below)]
            if xb >= 4:
                outer = [pltpu.roll(outer[0], 64, 1), pltpu.roll(outer[1], 192, 1)]
            ext_ref[xb, pl.ds(0, 8), :] = outer[0]
            ext_ref[xb, pl.ds(8, 24), :] = inner[0]
            ext_ref[xb, pl.ds(32, 64), :] = own_ref[xb].astype(F32)
            ext_ref[xb, pl.ds(96, 24), :] = inner[1]
            ext_ref[xb, pl.ds(120, 8), :] = outer[1]
        for p in range(4):
            at = (pl.ds(224 + 16 * (p // 2), 16), pl.ds(128 * (p % 2), 128))
            cot_ref[p, pl.ds(0, 16), :] = above[at]
            cot_ref[p, pl.ds(16, 64), :] = cown_ref[p]
            cot_ref[p, pl.ds(80, 16), :] = below[at]
        for k in range(2):
            marks_ref[pl.ds(16 * k, 16), :] = above[pl.ds(256, 16), pl.ds(0, 128)]
            marks_ref[pl.ds(96 + 16 * k, 16), :] = below[pl.ds(256, 16), pl.ds(0, 128)]

    marks_ref[pl.ds(32, 64), :] = jnp.full((64, 128), flag_ref[0].astype(F32), F32).astype(BF16)
    pl.when(odd_y == 1)(lambda: place(yb_ref, ya_ref))
    pl.when(odd_y == 0)(lambda: place(ya_ref, yb_ref))

    marks = marks_ref[...].astype(F32)[8:120]
    for k in range(NB):
        spread_block(p_ref, k, ext_ref[k])
    for n in range(2):
        places = [(p_ref, 4 * n + k) for k in range(4)]
        down_scr[n] = forward_pair(places, lambda b: marks, w1_ref, wd_ref, dv_ref, 2 * n, d_ref, n)

    def send(low, high):
        for ref, n, near, outer, lane in ((low, 0, 0, 1, 0), (high, 1, 7, 6, 128)):
            ref[pl.ds(0, 128), :] = ext_ref[near].astype(BF16)
            for h in range(2):
                half = pl.ds(128 * h, 128)
                ref[pl.ds(128, 64), half] = ext_ref[outer, pl.ds(64 * h, 64), pl.ds(lane, 128)].astype(BF16)
                ref[pl.ds(192, 48), half] = cot_ref[3 * n, pl.ds(48 * h, 48), :]
            ref[pl.ds(240, 64), pl.ds(0, 128)] = down_scr[n, pl.ds(0, 64), :]
            ref[pl.ds(240, 48), pl.ds(128, 128)] = down_scr[n, pl.ds(64, 48), :]
            ends = [marks_ref[pl.ds(96 * k, 16), :].astype(F32)[:8] for k in range(2)]
            own = marks_ref[pl.ds(32, 16), :].astype(F32)
            flags = jnp.where(low_y((16, 128)), jnp.concatenate(ends, axis=0), own)
            ref[pl.ds(288, 16), pl.ds(128, 128)] = flags.astype(BF16)

    pl.when(odd_x == 1)(lambda: send(second_ref, first_ref))
    pl.when(odd_x == 0)(lambda: send(first_ref, second_ref))


def middle_kernel(
    cot_ref, marks_ref, p_ref, d_ref, w1_ref, w3_ref, w4_ref, wd_ref, wu_ref,
    g_ref, q_ref,
    dv_scr, d_scr,
):
    marks = marks_ref[...].astype(F32)[8:120]
    places = [(p_ref, 2 + k) for k in range(4)]
    forward_pair(places, lambda b: marks, w1_ref, wd_ref, dv_scr, 0, d_scr, 0)
    places = [(d_ref, 0), (d_scr, 0), (d_ref, 1)]
    coarse_forward(places, lambda k: cot_ref[1 + k], w3_ref, g_ref, 0)
    grad = dot(pair_lhs((g_ref, 0), (g_ref, 1)), w4_ref[...]).astype(BF16)
    fine_gradient(grad, lambda b: dv_scr[b], wu_ref, q_ref, 0)


def side_steps(
    side, msg_ref, cot_ref, marks_ref, pe_ref, dve_ref, de_ref, gm_ref, qm_ref, q_ref, parity_ref,
    w1_ref, w2_ref, w3_ref, w4_ref, wd_ref, wu_ref,
    store_out, scratch,
):
    p_scr, flag_scr, dv_scr, d_scr, cot_scr, g_scr, q_scr = scratch
    other = 1 - side
    right = side.astype(F32)

    spread_block(p_scr, 1 + side, msg_ref[pl.ds(0, 128), :])
    half = [msg_ref[pl.ds(128, 64), pl.ds(128 * h, 128)] for h in range(2)]
    half = jnp.concatenate(half, axis=0).astype(F32)
    spread_block(p_scr, 3 * side, jnp.concatenate([half * right, half * (1.0 - right)], axis=1))
    for k in range(2):
        for m in range(4):
            p_scr[m, 2 * other + k] = pe_ref[m, 6 * side + k]
        dv_scr[2 * other + k] = dve_ref[2 * side + k]
    flags = msg_ref[pl.ds(288, 16), pl.ds(128, 128)].astype(F32)
    turned = pltpu.roll(flags, 64, 1)
    ends = jnp.where(low_y((16, 128)), flags, turned)
    own = jnp.where(low_y((16, 128)), turned, flags)
    flag_scr[side] = jnp.concatenate([ends[:8]] * 3 + [own] * 4 + [ends[8:]] * 3, axis=0)
    flag_scr[other] = marks_ref[...].astype(F32)[8:120]
    for h in range(2):
        cot_scr[side, pl.ds(48 * h, 48), :] = msg_ref[pl.ds(192, 48), pl.ds(128 * h, 128)]
    cot_scr[other] = cot_ref[3 * side]
    down = [msg_ref[pl.ds(240, 64 - 16 * h), pl.ds(128 * h, 128)] for h in range(2)]
    down = jnp.concatenate(down, axis=0).astype(F32)
    coarse_forms(down.reshape(14, 8, 128), storer(d_scr, 2 * side))
    for t in range(9):
        d_scr[t, 2 * other] = de_ref[t, side]
        g_scr[t, 2 * other] = gm_ref[t, side]
    for m in range(4):
        for k in range(2):
            q_scr[m, 4 * other + k] = qm_ref[m, k]

    places = [(p_scr, k) for k in range(4)]
    forward_pair(places, lambda b: flag_scr[b], w1_ref, wd_ref, dv_scr, 2 * side, d_scr, 1)
    coarse_forward([(d_scr, k) for k in range(3)], lambda k: cot_scr[k], w3_ref, g_scr, side)
    lhs = jnp.concatenate([pair_lhs((g_scr, k), (g_scr, k + 1)) for k in range(2)], axis=0)
    grad = dot(lhs, w4_ref[...]).astype(BF16)
    for k in range(2):
        fine_gradient(grad[80 * k : 80 * k + 80], lambda b: dv_scr[2 * k + b], wu_ref, q_scr, 2 * side + 2 * k)
    lhs = jnp.concatenate([conv_lhs(*((q_scr, k + n) for n in range(3))) for k in range(4)], axis=0)
    grad = dot(lhs, w2_ref[...]).astype(BF16)
    parity = parity_ref[...].astype(F32)
    for k in range(4):
        spread = lax.dot_general(grad[64 * k : 64 * k + 64], q_ref[...], TN, preferred_element_type=F32) * parity
        for b in range(2):
            rows = sum(spread[128 * b + 32 * i : 128 * b + 32 * i + 32] for i in range(4))
            store_out(2 * k + b, rows)


def near_kernel(msg_ref, *refs):
    inputs, out_ref, scratch = refs[:15], refs[15], refs[16:]

    def store_out(x, rows):
        for h in range(2):
            out_ref[h, pl.ds(x, C1, stride=8), :] = rows[:, 128 * h : 128 * h + 128]

    side_steps(1 - is_odd("gx"), msg_ref, *inputs, store_out, scratch)


def far_kernel(msg_ref, near_ref, *refs):
    inputs, out_ref, scratch, o_scr = refs[:15], refs[15], refs[16:-1], refs[-1]
    side = is_odd("gx")
    o_scr[1 - side] = near_ref[...]

    def store_out(x, rows):
        for h in range(2):
            o_scr[side, h, pl.ds(x, C1, stride=8), :] = rows[:, 128 * h : 128 * h + 128]

    side_steps(side, msg_ref, *inputs, store_out, scratch)
    halves = [jnp.concatenate([o_scr[n, h].reshape(32, 8, 128) for h in range(2)], axis=2) for n in range(2)]
    out_ref[...] = jnp.concatenate(halves, axis=1).astype(BF16)


SIDE_SCRATCH = [
    pltpu.VMEM((4, 4, 112, 256), BF16),
    pltpu.VMEM((2, 112, 128), F32),
    pltpu.VMEM((4, 80, 256), F32),
    pltpu.VMEM((9, 3, 96, 128), BF16),
    pltpu.VMEM((2, 96, 128), BF16),
    pltpu.VMEM((9, 3, 80, 128), BF16),
    pltpu.VMEM((4, 6, 64, 256), BF16),
]
VMEM = pl.BlockSpec(memory_space=pltpu.VMEM)
SMEM = pl.BlockSpec(memory_space=pltpu.SMEM)


def call(kernel, specs, outs, scratch, flops, nbytes, *args):
    return pl.pallas_call(
        kernel,
        out_shape=outs,
        in_specs=specs,
        out_specs=jax.tree.map(lambda _: VMEM, outs),
        scratch_shapes=scratch,
        compiler_params=pltpu.CompilerParams(vmem_limit_bytes=24 * 1024 * 1024),
        cost_estimate=pl.CostEstimate(flops=flops, bytes_accessed=nbytes, transcendentals=0),
    )(*args)


def shape(*dims, dtype=BF16):
    return jax.ShapeDtypeStruct(dims, dtype)


def swaps(first, second, axis):
    count = lax.axis_size(axis)

    def both_ways(start):
        edges = [(i, i + 1) for i in range(start, count - 1, 2)]
        return edges + [(j, i) for i, j in edges]

    return lax.ppermute(first, axis, both_ways(1)), lax.ppermute(second, axis, both_ways(0))


def on_device(features, brick_mask, kernel_fine, kernel_down, kernel_coarse, cotangent):
    flag = brick_mask.reshape(1)
    q, parity = call(constant_kernel, [], [shape(64, 256), shape(256, 256)], [], 4 * 10**9, 10**5)
    own, cown, y_first, y_second = call(
        pack_kernel,
        [SMEM] + [VMEM] * 4,
        [shape(8, 64, 256), shape(4, 64, 128), shape(YMSG, 256), shape(YMSG, 256)],
        [pltpu.VMEM((2, 512, 128), F32), pltpu.VMEM((512, 128), F32), pltpu.VMEM((2, YMSG, 256), BF16)],
        2 * 10**9, 10**6, flag, features, cotangent, q, parity,
    )
    y_a, y_b = swaps(y_first, y_second, "gy")
    w1, w2, w3, w4, wd, wu = call(
        weight_kernel,
        [VMEM] * 3,
        [shape(2048, 256), shape(2048, 256), shape(2304, 128), shape(2304, 128), shape(512, 128), shape(2, 128, 256)],
        [
            pltpu.VMEM((27, 32, 256), BF16),
            pltpu.VMEM((36, 32, 256), BF16),
            pltpu.VMEM((48, 32, 256), BF16),
            pltpu.VMEM((27, 64, 128), BF16),
        ],
        10**9, 10**7,
        kernel_fine.reshape(27 * C1, C1),
        kernel_coarse.reshape(27 * C2, C2),
        kernel_down.reshape(8 * C2, C1),
    )
    x_first, x_second, cot, marks, pe, dve, de = call(
        edge_kernel,
        [SMEM] + [VMEM] * 6,
        [
            shape(XMSG, 256), shape(XMSG, 256), shape(4, 96, 128), shape(128, 128),
            shape(4, 8, 112, 256), shape(4, 80, 256, dtype=F32), shape(9, 2, 96, 128),
        ],
        [pltpu.VMEM((8, 128, 256), F32), pltpu.VMEM((2, 112, 128), BF16)],
        5 * 10**8, 10**6, flag, own, cown, y_a, y_b, w1, wd,
    )
    x_a, x_b = swaps(x_first, x_second, "gx")
    gm, qm = call(
        middle_kernel,
        [VMEM] * 9,
        [shape(9, 2, 80, 128), shape(4, 2, 64, 256)],
        [pltpu.VMEM((2, 80, 256), F32), pltpu.VMEM((9, 1, 96, 128), BF16)],
        2 * 10**10, 10**7,
        cot, marks, pe, de, w1, w3, w4, wd, wu,
    )
    shared = (cot, marks, pe, dve, de, gm, qm, q, parity, w1, w2, w3, w4, wd, wu)
    near = call(
        near_kernel,
        [VMEM] * 16,
        shape(2, 256, 128, dtype=F32),
        SIDE_SCRATCH,
        2 * 10**10, 10**7, x_b, *shared,
    )
    return call(
        far_kernel,
        [VMEM] * 17,
        shape(32, 16, 256),
        SIDE_SCRATCH + [pltpu.VMEM((2, 2, 256, 128), F32)],
        10**10, 10**7, x_a, near, *shared,
    )


def solution(mesh):
    placed = (P(None, "gx", "gy"), P("gx", "gy", None), P(), P(), P(), P(None, "gx", "gy"))
    return jax.shard_map(
        on_device, mesh=mesh, in_specs=placed, out_specs=P(None, "gx", "gy"), check_vma=False
    )
```

```python
import jax
import jax.numpy as jnp
from jax import lax
from jax.experimental import pallas as pl
from jax.experimental.pallas import tpu as pltpu
from jax.sharding import PartitionSpec as P

C1 = 32
C2 = 64
LANES = 256
HALO = 4
NB = 8
WIDE = NB + 2 * HALO
YMSG = 192 + 32 + 32 + 16
XMSG = 192 + 48 + 64
F32 = jnp.float32
BF16 = jnp.bfloat16
NT = (((1,), (1,)), ((), ()))
TN = (((0,), (0,)), ((), ()))


def iota(shape, dim):
    return lax.broadcasted_iota(jnp.int32, shape, dim)


def one_hot(cond):
    return jnp.where(cond, 1.0, 0.0).astype(BF16)


def dot(a, b):
    return jnp.dot(a, b, preferred_element_type=F32)


def block_sum_matrix():
    r, l = iota((64, 256), 0), iota((64, 256), 1)
    return one_hot((r // 8 == l // 32) & (r % 8 == (l % 16) // 2))


def parity_matrix():
    r, l = iota((256, 256), 0), iota((256, 256), 1)
    return one_hot(((r // 64) % 2 == (l // 16) % 2) & ((r // 32) % 2 == l % 2))


def is_odd(axis):
    return lax.rem(lax.axis_index(axis), 2)


def constant_kernel(q_ref, parity_ref):
    q_ref[...] = block_sum_matrix()
    parity_ref[...] = parity_matrix()


def low_y(shape):
    return (iota(shape, len(shape) - 1) // 64) % 2 == 0


def pack_kernel(flag_ref, feat_ref, cot_ref, q_ref, parity_ref, own_ref, cown_ref, first_ref, second_ref, f_scr, c_scr, m_scr):
    odd = is_odd("gy")
    flag = flag_ref[0].astype(F32)
    cells = feat_ref[...].astype(F32).reshape(512, 256)
    f_scr[0] = cells[:, :128]
    f_scr[1] = cells[:, 128:]
    c_scr[:, :64] = cot_ref[...].astype(F32).reshape(512, 64) * flag
    parity = parity_ref[...]
    blocks = []
    for xb in range(NB):
        parts = []
        for a0 in range(2):
            at = pl.ds(2 * xb + a0, C1, stride=16)
            rows = jnp.concatenate([f_scr[0, at, :], f_scr[1, at, :]], axis=1).astype(BF16)
            parts += [rows] * 4
        spread = jnp.concatenate(parts, axis=0) * parity
        blocks.append(lax.dot_general(q_ref[...], spread, NT, preferred_element_type=F32))
        own_ref[xb] = blocks[xb].astype(BF16)
    for n, (inner, outer) in enumerate(((0, 24), (40, 32))):
        for j in range(4):
            rows = [blocks[2 * j + k][inner : inner + 24] for k in range(2)]
            m_scr[n, pl.ds(48 * j, 48), :] = jnp.concatenate(rows, axis=0).astype(BF16)
        rows = []
        for k in range(4):
            here, there = (blocks[k + i][outer : outer + 8] for i in (0, 4))
            there = pltpu.roll(there, 64 if n == 0 else 192, 1)
            low = low_y((8, 256))
            rows.append(jnp.where(low, here, there) if n == 0 else jnp.where(low, there, here))
        m_scr[n, pl.ds(192, 32), :] = jnp.concatenate(rows, axis=0).astype(BF16)
        m_scr[n, pl.ds(256, 16), :] = jnp.full((16, LANES), flag, F32).astype(BF16)
    eye = one_hot(iota((64, 64), 0) == iota((64, 64), 1))
    for p in range(4):
        rows = jnp.concatenate(
            [c_scr[pl.ds(2 * p + b, C2, stride=8), :] for b in range(2)], axis=0
        )[:, :64].astype(BF16)
        cells = lax.dot_general(eye, rows, NT, preferred_element_type=F32).astype(BF16)
        cown_ref[p] = cells
        at = (pl.ds(224 + 16 * (p // 2), 16), pl.ds(128 * (p % 2), 128))
        m_scr[(0, *at)] = cells[:16]
        m_scr[(1, *at)] = cells[48:]
    first_ref[...] = m_scr[odd]
    second_ref[...] = m_scr[1 - odd]


OFFSETS = {(0, 0): 0, (1, 0): 1, (0, 1): 2, (1, 1): -1}


def fine_weights(u_ref, out_ref, u_scr, v_scr, w_scr, backward):
    tile = one_hot(iota((32, 256), 0) == iota((32, 256), 1) % 32)
    taps_in = u_ref[...]
    if not backward:
        eye = one_hot(iota((32, 32), 0) == iota((32, 32), 1))
        turned = lax.dot_general(eye, taps_in, NT, preferred_element_type=F32)
        taps_in = jnp.concatenate([turned[:, 32 * e : 32 * e + 32] for e in range(27)], axis=0).astype(BF16)
    u_scr[...] = dot(taps_in, tile).astype(BF16).reshape(27, 32, 256)
    lane = iota((32, 256), 1)
    low2 = one_hot((lane // 32) % 2 == 0), one_hot((lane // 32) % 2 == 1)
    low1 = one_hot((lane // 64) % 2 == 0), one_hot((lane // 64) % 2 == 1)

    def taps(f):
        return ((-f, 1 - f) if backward else (f, f - 1))

    def mix(load, f, masks):
        terms = [load(e) * mask for e, mask in zip(taps(f), masks) if abs(e) <= 1]
        return sum(terms[1:], terms[0])

    def body(e0, carry):
        for e1 in range(3):
            for f2 in range(-1, 3):
                v_scr[e0 * 12 + e1 * 4 + (f2 + 1)] = mix(
                    lambda e2: u_scr[e0 * 9 + e1 * 3 + e2 + 1], f2, low2
                )
        for f1 in range(-1, 3):
            for f2 in range(-1, 3):
                w_scr[e0 * 16 + (f1 + 1) * 4 + f2 + 1] = mix(
                    lambda e1: v_scr[e0 * 12 + (e1 + 1) * 4 + f2 + 1], f1, low1
                )
        return carry

    lax.fori_loop(0, 3, body, 0)
    half = jnp.zeros((32, 128), BF16)
    for my in range(2):
        for mz in range(2):
            for mx in range(2):
                for a0 in range(2):
                    for a1 in range(2):
                        for a2 in range(2):
                            f0, f1, f2 = OFFSETS[a0, mx], OFFSETS[a1, my], OFFSETS[a2, mz]
                            row = ((my * 2 + mz) * 2 + mx) * 256 + (a0 * 4 + a1 * 2 + a2) * 32
                            for b0, e0 in enumerate(taps(f0)):
                                at = (pl.ds(row, 32), pl.ds(128 * b0, 128))
                                if abs(e0) <= 1:
                                    out_ref[at] = w_scr[(e0 + 1) * 16 + (f1 + 1) * 4 + f2 + 1, :, 128 * b0 : 128 * b0 + 128]
                                else:
                                    out_ref[at] = half


def coarse_weights(u_ref, out_ref, u_scr, backward):
    if backward:
        tile = one_hot(iota((64, 128), 0) == iota((64, 128), 1) % 64)
        u_scr[...] = dot(u_ref[...], tile).astype(BF16).reshape(27, 64, 128)
    else:
        eye = one_hot(iota((64, 64), 0) == iota((64, 64), 1))
        for e in range(27):
            turned = lax.dot_general(eye, u_ref[pl.ds(64 * e, 64), :], NT, preferred_element_type=F32)
            u_scr[e] = jnp.concatenate([turned, turned], axis=1).astype(BF16)
    masks = one_hot(iota((64, 128), 1) < 64), one_hot(iota((64, 128), 1) >= 64)

    def body(t, carry):
        k = 8 - t if backward else t
        for s in range(4):
            taps = (1 - s, 2 - s) if backward else (s - 1, s - 2)
            terms = [u_scr[(e + 1) * 9 + k] * mask for e, mask in zip(taps, masks) if abs(e) <= 1]
            out_ref[pl.ds(t * 256 + s * 64, 64), :] = sum(terms[1:], terms[0])
        return carry

    lax.fori_loop(0, 9, body, 0)


def weight_kernel(
    u1_ref, u2_ref, ud_ref,
    w1_ref, w2_ref, w3_ref, w4_ref, wd_ref, wu_ref,
    u_scr, v_scr, w_scr, uc_scr,
):
    fine_weights(u1_ref, w1_ref, u_scr, v_scr, w_scr, False)
    fine_weights(u1_ref, w2_ref, u_scr, v_scr, w_scr, True)
    coarse_weights(u2_ref, w3_ref, uc_scr, False)
    coarse_weights(u2_ref, w4_ref, uc_scr, True)
    lane = iota((32, 256), 1)
    up = sum(
        dot(ud_ref[pl.ds(64 * a, 64), :], one_hot(iota((32, 256), 0) + 32 * a == lane)) for a in range(8)
    ).astype(BF16)
    for b in range(2):
        place = one_hot(iota((64, 128), 0) + 64 * b == iota((64, 128), 1))
        turned = lax.dot_general(up, place, TN, preferred_element_type=F32)
        wd_ref[pl.ds(256 * b, 256), :] = turned.astype(BF16)
        wu_ref[b, pl.ds(64 * b, 64), :] = up
        wu_ref[b, pl.ds(64 * (1 - b), 64), :] = jnp.zeros((64, 256), BF16)


def silu_parts(v):
    s = 0.5 + 0.5 * jnp.tanh(0.5 * v)
    vs = v * s
    return vs, s + vs * (1.0 - s)


def keep(shape, cond):
    return jnp.where(cond(iota(shape, 1), iota(shape, 2)), 1.0, 0.0)


def shift_z(cells, up):
    shape = (1, *cells.shape[1:])
    if up:
        return pltpu.roll(cells, 7, 1) * keep(shape, lambda z, lane: z < 7)
    return pltpu.roll(cells, 1, 1) * keep(shape, lambda z, lane: z > 0)


def mixed(cells, store):
    n = cells.shape[0]
    rows = (n - 2) * 8
    low = keep((1, 8, 256), lambda z, lane: ((lane // 32) % 2 == 0) & (z < 7))
    high = keep((1, 8, 256), lambda z, lane: ((lane // 32) % 2 == 1) & (z > 0))
    zmix = pltpu.roll(cells, 7, 1) * low + pltpu.roll(cells, 1, 1) * high
    low1 = (iota((n - 2, 8, 256), 2) // 64) % 2 == 0
    for mz, form in enumerate((cells, zmix)):
        store(mz, form[1 : n - 1].reshape(rows, 256).astype(BF16))
        store(2 + mz, jnp.where(low1, form[2:], form[: n - 2]).reshape(rows, 256).astype(BF16))


def conv_lhs(before, here, after):
    parts = []
    for m in range(4):
        parts += [here[0][m, here[1]], after[0][m, after[1], :, :128], before[0][m, before[1], :, 128:]]
    return jnp.concatenate(parts, axis=1)


def coarse_forms(cells, store):
    n = cells.shape[0]
    for dz, form in enumerate((shift_z(cells, False), cells, shift_z(cells, True))):
        for dy in range(3):
            store(dy * 3 + dz, form[dy : dy + n - 2].reshape((n - 2) * 8, 128).astype(BF16))


def storer(scr, slot):
    def store(m, value):
        scr[m, slot] = value

    return store


def pair_lhs(low, high):
    parts = []
    for t in range(9):
        parts += [low[0][t, low[1]], high[0][t, high[1]]]
    return jnp.concatenate(parts, axis=1)


def spread_block(p_scr, slot, cells):
    mixed(cells.astype(F32).reshape(16, 8, 256), storer(p_scr, slot))


def forward_pair(places, marks, w1_ref, wd_ref, dv_scr, dv_slot, d_scr, d_slot):
    lhs = jnp.concatenate([conv_lhs(*places[:3]), conv_lhs(*places[1:])], axis=0)
    pre = dot(lhs, w1_ref[...])
    hidden = []
    for b in range(2):
        value, slope = silu_parts(pre[112 * b : 112 * b + 112])
        flags = jnp.concatenate([marks(b)] * 2, axis=1)
        hidden.append((flags * value).astype(BF16))
        dv_scr[dv_slot + b] = (flags * slope)[16:96]
    down = dot(jnp.concatenate(hidden, axis=1), wd_ref[...]).astype(BF16)
    coarse_forms(down.astype(F32).reshape(14, 8, 128), storer(d_scr, d_slot))
    return down


def coarse_forward(places, cots, w3_ref, g_scr, g_first):
    lhs = jnp.concatenate([pair_lhs(*places[:2]), pair_lhs(*places[1:])], axis=0)
    pre = dot(lhs, w3_ref[...])
    for k in range(2):
        _, slope = silu_parts(pre[96 * k : 96 * k + 96])
        grad = (cots(k).astype(F32) * slope).astype(BF16)
        coarse_forms(grad.astype(F32).reshape(12, 8, 128), storer(g_scr, g_first + k))


def fine_gradient(grad, slopes, wu_ref, q_scr, slot):
    for b in range(2):
        fine = (dot(grad, wu_ref[b]) * slopes(b)).astype(BF16)
        mixed(fine.astype(F32).reshape(10, 8, 256), storer(q_scr, slot + b))


def edge_kernel(
    flag_ref, own_ref, cown_ref, ya_ref, yb_ref, w1_ref, wd_ref,
    first_ref, second_ref, cot_ref, marks_ref, p_ref, dv_ref, d_ref,
    ext_ref, down_scr,
):
    odd_y, odd_x = is_odd("gy"), is_odd("gx")

    def place(above, below):
        for xb in range(NB):
            at = 48 * (xb // 2), 24 * (xb % 2)
            inner = [ref[pl.ds(at[0], 48), :].astype(F32)[at[1] : at[1] + 24] for ref in (above, below)]
            at = 192 + 16 * ((xb % 4) // 2), 8 * (xb % 2)
            outer = [ref[pl.ds(at[0], 16), :].astype(F32)[at[1] : at[1] + 8] for ref in (above, below)]
            if xb >= 4:
                outer = [pltpu.roll(outer[0], 64, 1), pltpu.roll(outer[1], 192, 1)]
            ext_ref[xb, pl.ds(0, 8), :] = outer[0]
            ext_ref[xb, pl.ds(8, 24), :] = inner[0]
            ext_ref[xb, pl.ds(32, 64), :] = own_ref[xb].astype(F32)
            ext_ref[xb, pl.ds(96, 24), :] = inner[1]
            ext_ref[xb, pl.ds(120, 8), :] = outer[1]
        for p in range(4):
            at = (pl.ds(224 + 16 * (p // 2), 16), pl.ds(128 * (p % 2), 128))
            cot_ref[p, pl.ds(0, 16), :] = above[at]
            cot_ref[p, pl.ds(16, 64), :] = cown_ref[p]
            cot_ref[p, pl.ds(80, 16), :] = below[at]
        for k in range(2):
            marks_ref[pl.ds(16 * k, 16), :] = above[pl.ds(256, 16), pl.ds(0, 128)]
            marks_ref[pl.ds(96 + 16 * k, 16), :] = below[pl.ds(256, 16), pl.ds(0, 128)]

    marks_ref[pl.ds(32, 64), :] = jnp.full((64, 128), flag_ref[0].astype(F32), F32).astype(BF16)
    pl.when(odd_y == 1)(lambda: place(yb_ref, ya_ref))
    pl.when(odd_y == 0)(lambda: place(ya_ref, yb_ref))

    marks = marks_ref[...].astype(F32)[8:120]
    for k in range(NB):
        spread_block(p_ref, k, ext_ref[k])
    for n in range(2):
        places = [(p_ref, 4 * n + k) for k in range(4)]
        down_scr[n] = forward_pair(places, lambda b: marks, w1_ref, wd_ref, dv_ref, 2 * n, d_ref, n)

    def send(low, high):
        for ref, n, near, outer, lane in ((low, 0, 0, 1, 0), (high, 1, 7, 6, 128)):
            ref[pl.ds(0, 128), :] = ext_ref[near].astype(BF16)
            for h in range(2):
                half = pl.ds(128 * h, 128)
                ref[pl.ds(128, 64), half] = ext_ref[outer, pl.ds(64 * h, 64), pl.ds(lane, 128)].astype(BF16)
                ref[pl.ds(192, 48), half] = cot_ref[3 * n, pl.ds(48 * h, 48), :]
            ref[pl.ds(240, 64), pl.ds(0, 128)] = down_scr[n, pl.ds(0, 64), :]
            ref[pl.ds(240, 48), pl.ds(128, 128)] = down_scr[n, pl.ds(64, 48), :]
            ends = [marks_ref[pl.ds(96 * k, 16), :].astype(F32)[:8] for k in range(2)]
            own = marks_ref[pl.ds(32, 16), :].astype(F32)
            flags = jnp.where(low_y((16, 128)), jnp.concatenate(ends, axis=0), own)
            ref[pl.ds(288, 16), pl.ds(128, 128)] = flags.astype(BF16)

    pl.when(odd_x == 1)(lambda: send(second_ref, first_ref))
    pl.when(odd_x == 0)(lambda: send(first_ref, second_ref))


def middle_kernel(
    cot_ref, marks_ref, p_ref, d_ref, w1_ref, w3_ref, w4_ref, wd_ref, wu_ref,
    g_ref, q_ref,
    dv_scr, d_scr,
):
    marks = marks_ref[...].astype(F32)[8:120]
    places = [(p_ref, 2 + k) for k in range(4)]
    forward_pair(places, lambda b: marks, w1_ref, wd_ref, dv_scr, 0, d_scr, 0)
    places = [(d_ref, 0), (d_scr, 0), (d_ref, 1)]
    coarse_forward(places, lambda k: cot_ref[1 + k], w3_ref, g_ref, 0)
    grad = dot(pair_lhs((g_ref, 0), (g_ref, 1)), w4_ref[...]).astype(BF16)
    fine_gradient(grad, lambda b: dv_scr[b], wu_ref, q_ref, 0)


def side_steps(
    side, msg_ref, cot_ref, marks_ref, pe_ref, dve_ref, de_ref, gm_ref, qm_ref, q_ref,
    w1_ref, w2_ref, w3_ref, w4_ref, wd_ref, wu_ref,
    store_out, scratch,
):
    p_scr, flag_scr, dv_scr, d_scr, cot_scr, g_scr, q_scr = scratch
    other = 1 - side
    right = side.astype(F32)

    spread_block(p_scr, 1 + side, msg_ref[pl.ds(0, 128), :])
    half = [msg_ref[pl.ds(128, 64), pl.ds(128 * h, 128)] for h in range(2)]
    half = jnp.concatenate(half, axis=0).astype(F32)
    spread_block(p_scr, 3 * side, jnp.concatenate([half * right, half * (1.0 - right)], axis=1))
    for k in range(2):
        for m in range(4):
            p_scr[m, 2 * other + k] = pe_ref[m, 6 * side + k]
        dv_scr[2 * other + k] = dve_ref[2 * side + k]
    flags = msg_ref[pl.ds(288, 16), pl.ds(128, 128)].astype(F32)
    turned = pltpu.roll(flags, 64, 1)
    ends = jnp.where(low_y((16, 128)), flags, turned)
    own = jnp.where(low_y((16, 128)), turned, flags)
    flag_scr[side] = jnp.concatenate([ends[:8]] * 3 + [own] * 4 + [ends[8:]] * 3, axis=0)
    flag_scr[other] = marks_ref[...].astype(F32)[8:120]
    for h in range(2):
        cot_scr[side, pl.ds(48 * h, 48), :] = msg_ref[pl.ds(192, 48), pl.ds(128 * h, 128)]
    cot_scr[other] = cot_ref[3 * side]
    down = [msg_ref[pl.ds(240, 64 - 16 * h), pl.ds(128 * h, 128)] for h in range(2)]
    down = jnp.concatenate(down, axis=0).astype(F32)
    coarse_forms(down.reshape(14, 8, 128), storer(d_scr, 2 * side))
    for t in range(9):
        d_scr[t, 2 * other] = de_ref[t, side]
        g_scr[t, 2 * other] = gm_ref[t, side]
    for m in range(4):
        for k in range(2):
            q_scr[m, 4 * other + k] = qm_ref[m, k]

    places = [(p_scr, k) for k in range(4)]
    forward_pair(places, lambda b: flag_scr[b], w1_ref, wd_ref, dv_scr, 2 * side, d_scr, 1)
    coarse_forward([(d_scr, k) for k in range(3)], lambda k: cot_scr[k], w3_ref, g_scr, side)
    lhs = jnp.concatenate([pair_lhs((g_scr, k), (g_scr, k + 1)) for k in range(2)], axis=0)
    grad = dot(lhs, w4_ref[...]).astype(BF16)
    for k in range(2):
        fine_gradient(grad[80 * k : 80 * k + 80], lambda b: dv_scr[2 * k + b], wu_ref, q_scr, 2 * side + 2 * k)
    lane = iota((32, 256), 1)
    low_y_cell, low_z_cell = (lane // 16) % 2 == 0, lane % 2 == 0
    for h in range(2):
        lhs = jnp.concatenate(
            [conv_lhs(*((q_scr, 2 * h + k + n) for n in range(3))) for k in range(2)], axis=0
        )
        grad = dot(lhs, w2_ref[...]).astype(BF16)
        for k in range(2):
            spread = lax.dot_general(grad[64 * k : 64 * k + 64], q_ref[...], TN, preferred_element_type=F32)
            for b in range(2):
                rows = [spread[128 * b + 32 * i : 128 * b + 32 * i + 32] for i in range(4)]
                pairs = [jnp.where(low_z_cell, rows[i], rows[i + 1]) for i in (0, 2)]
                store_out(4 * h + 2 * k + b, jnp.where(low_y_cell, *pairs))


def near_kernel(msg_ref, *refs):
    inputs, out_ref, scratch = refs[:14], refs[14], refs[15:]

    def store_out(x, rows):
        for h in range(2):
            out_ref[h, pl.ds(x, C1, stride=8), :] = rows[:, 128 * h : 128 * h + 128]

    side_steps(1 - is_odd("gx"), msg_ref, *inputs, store_out, scratch)


def far_kernel(msg_ref, near_ref, *refs):
    inputs, out_ref, scratch, o_scr = refs[:14], refs[14], refs[15:-1], refs[-1]
    side = is_odd("gx")
    o_scr[1 - side] = near_ref[...]

    def store_out(x, rows):
        for h in range(2):
            o_scr[side, h, pl.ds(x, C1, stride=8), :] = rows[:, 128 * h : 128 * h + 128]

    side_steps(side, msg_ref, *inputs, store_out, scratch)
    halves = [jnp.concatenate([o_scr[n, h].reshape(32, 8, 128) for h in range(2)], axis=2) for n in range(2)]
    out_ref[...] = jnp.concatenate(halves, axis=1).astype(BF16)


SIDE_SCRATCH = [
    pltpu.VMEM((4, 4, 112, 256), BF16),
    pltpu.VMEM((2, 112, 128), F32),
    pltpu.VMEM((4, 80, 256), F32),
    pltpu.VMEM((9, 3, 96, 128), BF16),
    pltpu.VMEM((2, 96, 128), BF16),
    pltpu.VMEM((9, 3, 80, 128), BF16),
    pltpu.VMEM((4, 6, 64, 256), BF16),
]
VMEM = pl.BlockSpec(memory_space=pltpu.VMEM)
SMEM = pl.BlockSpec(memory_space=pltpu.SMEM)


def call(kernel, specs, outs, scratch, flops, nbytes, *args):
    return pl.pallas_call(
        kernel,
        out_shape=outs,
        in_specs=specs,
        out_specs=jax.tree.map(lambda _: VMEM, outs),
        scratch_shapes=scratch,
        compiler_params=pltpu.CompilerParams(vmem_limit_bytes=24 * 1024 * 1024),
        cost_estimate=pl.CostEstimate(flops=flops, bytes_accessed=nbytes, transcendentals=0),
    )(*args)


def shape(*dims, dtype=BF16):
    return jax.ShapeDtypeStruct(dims, dtype)


def swaps(first, second, axis):
    count = lax.axis_size(axis)

    def both_ways(start):
        edges = [(i, i + 1) for i in range(start, count - 1, 2)]
        return edges + [(j, i) for i, j in edges]

    return lax.ppermute(first, axis, both_ways(1)), lax.ppermute(second, axis, both_ways(0))


def on_device(features, brick_mask, kernel_fine, kernel_down, kernel_coarse, cotangent):
    flag = brick_mask.reshape(1)
    q, parity = call(constant_kernel, [], [shape(64, 256), shape(256, 256)], [], 4 * 10**9, 10**5)
    own, cown, y_first, y_second = call(
        pack_kernel,
        [SMEM] + [VMEM] * 4,
        [shape(8, 64, 256), shape(4, 64, 128), shape(YMSG, 256), shape(YMSG, 256)],
        [pltpu.VMEM((2, 512, 128), F32), pltpu.VMEM((512, 128), F32), pltpu.VMEM((2, YMSG, 256), BF16)],
        2 * 10**9, 10**6, flag, features, cotangent, q, parity,
    )
    y_a, y_b = swaps(y_first, y_second, "gy")
    w1, w2, w3, w4, wd, wu = call(
        weight_kernel,
        [VMEM] * 3,
        [shape(2048, 256), shape(2048, 256), shape(2304, 128), shape(2304, 128), shape(512, 128), shape(2, 128, 256)],
        [
            pltpu.VMEM((27, 32, 256), BF16),
            pltpu.VMEM((36, 32, 256), BF16),
            pltpu.VMEM((48, 32, 256), BF16),
            pltpu.VMEM((27, 64, 128), BF16),
        ],
        10**9, 10**7,
        kernel_fine.reshape(27 * C1, C1),
        kernel_coarse.reshape(27 * C2, C2),
        kernel_down.reshape(8 * C2, C1),
    )
    x_first, x_second, cot, marks, pe, dve, de = call(
        edge_kernel,
        [SMEM] + [VMEM] * 6,
        [
            shape(XMSG, 256), shape(XMSG, 256), shape(4, 96, 128), shape(128, 128),
            shape(4, 8, 112, 256), shape(4, 80, 256, dtype=F32), shape(9, 2, 96, 128),
        ],
        [pltpu.VMEM((8, 128, 256), F32), pltpu.VMEM((2, 112, 128), BF16)],
        5 * 10**8, 10**6, flag, own, cown, y_a, y_b, w1, wd,
    )
    x_a, x_b = swaps(x_first, x_second, "gx")
    gm, qm = call(
        middle_kernel,
        [VMEM] * 9,
        [shape(9, 2, 80, 128), shape(4, 2, 64, 256)],
        [pltpu.VMEM((2, 80, 256), F32), pltpu.VMEM((9, 1, 96, 128), BF16)],
        2 * 10**10, 10**7,
        cot, marks, pe, de, w1, w3, w4, wd, wu,
    )
    shared = (cot, marks, pe, dve, de, gm, qm, q, w1, w2, w3, w4, wd, wu)
    near = call(
        near_kernel,
        [VMEM] * 15,
        shape(2, 256, 128, dtype=F32),
        SIDE_SCRATCH,
        2 * 10**10, 10**7, x_b, *shared,
    )
    return call(
        far_kernel,
        [VMEM] * 16,
        shape(32, 16, 256),
        SIDE_SCRATCH + [pltpu.VMEM((2, 2, 256, 128), F32)],
        10**10, 10**7, x_a, near, *shared,
    )


def solution(mesh):
    placed = (P(None, "gx", "gy"), P("gx", "gy", None), P(), P(), P(), P(None, "gx", "gy"))
    return jax.shard_map(
        on_device, mesh=mesh, in_specs=placed, out_specs=P(None, "gx", "gy"), check_vma=False
    )
```

```python
import jax
import jax.numpy as jnp
from jax import lax
from jax.experimental import pallas as pl
from jax.experimental.pallas import tpu as pltpu
from jax.sharding import PartitionSpec as P

C1 = 32
C2 = 64
LANES = 256
HALO = 4
NB = 8
WIDE = NB + 2 * HALO
YMSG = 192 + 32 + 32 + 16
XMSG = 192 + 48 + 64
F32 = jnp.float32
BF16 = jnp.bfloat16
NT = (((1,), (1,)), ((), ()))
TN = (((0,), (0,)), ((), ()))


def iota(shape, dim):
    return lax.broadcasted_iota(jnp.int32, shape, dim)


def one_hot(cond):
    return jnp.where(cond, 1.0, 0.0).astype(BF16)


def dot(a, b):
    return jnp.dot(a, b, preferred_element_type=F32)


def block_sum_matrix():
    r, l = iota((64, 256), 0), iota((64, 256), 1)
    return one_hot((r // 8 == l // 32) & (r % 8 == (l % 16) // 2))


def parity_matrix():
    r, l = iota((256, 256), 0), iota((256, 256), 1)
    return one_hot(((r // 64) % 2 == (l // 16) % 2) & ((r // 32) % 2 == l % 2))


def is_odd(axis):
    return lax.rem(lax.axis_index(axis), 2)


def constant_kernel(q_ref, parity_ref):
    q_ref[...] = block_sum_matrix()
    parity_ref[...] = parity_matrix()


def low_y(shape):
    return (iota(shape, len(shape) - 1) // 64) % 2 == 0


def pack_kernel(flag_ref, feat_ref, cot_ref, q_ref, parity_ref, own_ref, cown_ref, first_ref, second_ref, f_scr, c_scr, m_scr):
    odd = is_odd("gy")
    flag = flag_ref[0].astype(F32)
    cells = feat_ref[...].astype(F32).reshape(512, 256)
    f_scr[0] = cells[:, :128]
    f_scr[1] = cells[:, 128:]
    c_scr[:, :64] = cot_ref[...].astype(F32).reshape(512, 64) * flag
    parity = parity_ref[...]
    blocks = []
    for xb in range(NB):
        parts = []
        for a0 in range(2):
            at = pl.ds(2 * xb + a0, C1, stride=16)
            rows = jnp.concatenate([f_scr[0, at, :], f_scr[1, at, :]], axis=1).astype(BF16)
            parts += [rows] * 4
        spread = jnp.concatenate(parts, axis=0) * parity
        blocks.append(lax.dot_general(q_ref[...], spread, NT, preferred_element_type=F32))
        own_ref[xb] = blocks[xb].astype(BF16)
    for n, (inner, outer) in enumerate(((0, 24), (40, 32))):
        for j in range(4):
            rows = [blocks[2 * j + k][inner : inner + 24] for k in range(2)]
            m_scr[n, pl.ds(48 * j, 48), :] = jnp.concatenate(rows, axis=0).astype(BF16)
        rows = []
        for k in range(4):
            here, there = (blocks[k + i][outer : outer + 8] for i in (0, 4))
            there = pltpu.roll(there, 64 if n == 0 else 192, 1)
            low = low_y((8, 256))
            rows.append(jnp.where(low, here, there) if n == 0 else jnp.where(low, there, here))
        m_scr[n, pl.ds(192, 32), :] = jnp.concatenate(rows, axis=0).astype(BF16)
        m_scr[n, pl.ds(256, 16), :] = jnp.full((16, LANES), flag, F32).astype(BF16)
    eye = one_hot(iota((64, 64), 0) == iota((64, 64), 1))
    for p in range(4):
        rows = jnp.concatenate(
            [c_scr[pl.ds(2 * p + b, C2, stride=8), :] for b in range(2)], axis=0
        )[:, :64].astype(BF16)
        cells = lax.dot_general(eye, rows, NT, preferred_element_type=F32).astype(BF16)
        cown_ref[p] = cells
        at = (pl.ds(224 + 16 * (p // 2), 16), pl.ds(128 * (p % 2), 128))
        m_scr[(0, *at)] = cells[:16]
        m_scr[(1, *at)] = cells[48:]
    first_ref[...] = m_scr[odd]
    second_ref[...] = m_scr[1 - odd]


OFFSETS = {(0, 0): 0, (1, 0): 1, (0, 1): 2, (1, 1): -1}


def fine_weights(u_ref, out_ref, u_scr, v_scr, w_scr, backward):
    tile = one_hot(iota((32, 256), 0) == iota((32, 256), 1) % 32)
    taps_in = u_ref[...]
    if not backward:
        eye = one_hot(iota((32, 32), 0) == iota((32, 32), 1))
        turned = lax.dot_general(eye, taps_in, NT, preferred_element_type=F32)
        taps_in = jnp.concatenate([turned[:, 32 * e : 32 * e + 32] for e in range(27)], axis=0).astype(BF16)
    u_scr[...] = dot(taps_in, tile).astype(BF16).reshape(27, 32, 256)
    lane = iota((32, 256), 1)
    low2 = one_hot((lane // 32) % 2 == 0), one_hot((lane // 32) % 2 == 1)
    low1 = one_hot((lane // 64) % 2 == 0), one_hot((lane // 64) % 2 == 1)

    def taps(f):
        return ((-f, 1 - f) if backward else (f, f - 1))

    def mix(load, f, masks):
        terms = [load(e) * mask for e, mask in zip(taps(f), masks) if abs(e) <= 1]
        return sum(terms[1:], terms[0])

    def body(e0, carry):
        for e1 in range(3):
            for f2 in range(-1, 3):
                v_scr[e0 * 12 + e1 * 4 + (f2 + 1)] = mix(
                    lambda e2: u_scr[e0 * 9 + e1 * 3 + e2 + 1], f2, low2
                )
        for f1 in range(-1, 3):
            for f2 in range(-1, 3):
                w_scr[e0 * 16 + (f1 + 1) * 4 + f2 + 1] = mix(
                    lambda e1: v_scr[e0 * 12 + (e1 + 1) * 4 + f2 + 1], f1, low1
                )
        return carry

    lax.fori_loop(0, 3, body, 0)
    half = jnp.zeros((32, 128), BF16)
    for my in range(2):
        for mz in range(2):
            for mx in range(2):
                for a0 in range(2):
                    for a1 in range(2):
                        for a2 in range(2):
                            f0, f1, f2 = OFFSETS[a0, mx], OFFSETS[a1, my], OFFSETS[a2, mz]
                            row = ((my * 2 + mz) * 2 + mx) * 256 + (a0 * 4 + a1 * 2 + a2) * 32
                            for b0, e0 in enumerate(taps(f0)):
                                at = (pl.ds(row, 32), pl.ds(128 * b0, 128))
                                if abs(e0) <= 1:
                                    out_ref[at] = w_scr[(e0 + 1) * 16 + (f1 + 1) * 4 + f2 + 1, :, 128 * b0 : 128 * b0 + 128]
                                else:
                                    out_ref[at] = half


def coarse_weights(u_ref, out_ref, u_scr, backward):
    if backward:
        tile = one_hot(iota((64, 128), 0) == iota((64, 128), 1) % 64)
        u_scr[...] = dot(u_ref[...], tile).astype(BF16).reshape(27, 64, 128)
    else:
        eye = one_hot(iota((64, 64), 0) == iota((64, 64), 1))
        for e in range(27):
            turned = lax.dot_general(eye, u_ref[pl.ds(64 * e, 64), :], NT, preferred_element_type=F32)
            u_scr[e] = jnp.concatenate([turned, turned], axis=1).astype(BF16)
    masks = one_hot(iota((64, 128), 1) < 64), one_hot(iota((64, 128), 1) >= 64)

    def body(t, carry):
        k = 8 - t if backward else t
        for s in range(4):
            taps = (1 - s, 2 - s) if backward else (s - 1, s - 2)
            terms = [u_scr[(e + 1) * 9 + k] * mask for e, mask in zip(taps, masks) if abs(e) <= 1]
            out_ref[pl.ds(t * 256 + s * 64, 64), :] = sum(terms[1:], terms[0])
        return carry

    lax.fori_loop(0, 9, body, 0)


def weight_kernel(
    u1_ref, u2_ref, ud_ref,
    w1_ref, w2_ref, w3_ref, w4_ref, wd_ref, wu_ref,
    u_scr, v_scr, w_scr, uc_scr,
):
    fine_weights(u1_ref, w1_ref, u_scr, v_scr, w_scr, False)
    fine_weights(u1_ref, w2_ref, u_scr, v_scr, w_scr, True)
    coarse_weights(u2_ref, w3_ref, uc_scr, False)
    coarse_weights(u2_ref, w4_ref, uc_scr, True)
    lane = iota((32, 256), 1)
    up = sum(
        dot(ud_ref[pl.ds(64 * a, 64), :], one_hot(iota((32, 256), 0) + 32 * a == lane)) for a in range(8)
    ).astype(BF16)
    for b in range(2):
        place = one_hot(iota((64, 128), 0) + 64 * b == iota((64, 128), 1))
        turned = lax.dot_general(up, place, TN, preferred_element_type=F32)
        wd_ref[pl.ds(256 * b, 256), :] = turned.astype(BF16)
        wu_ref[b, pl.ds(64 * b, 64), :] = up
        wu_ref[b, pl.ds(64 * (1 - b), 64), :] = jnp.zeros((64, 256), BF16)


def silu_parts(v):
    s = 0.5 + 0.5 * jnp.tanh(0.5 * v)
    vs = v * s
    return vs, s + vs * (1.0 - s)


def shift_z(cells, up):
    z = iota(cells.shape, 1)
    if up:
        return jnp.where(z < 7, pltpu.roll(cells, 7, 1), 0.0)
    return jnp.where(z > 0, pltpu.roll(cells, 1, 1), 0.0)


def mixed(cells, store):
    n = cells.shape[0]
    rows = (n - 2) * 8
    lane = iota(cells.shape, 2)
    zmix = jnp.where((lane // 32) % 2 == 0, shift_z(cells, True), shift_z(cells, False))
    low1 = (iota((n - 2, 8, 256), 2) // 64) % 2 == 0
    for mz, form in enumerate((cells, zmix)):
        store(mz, form[1 : n - 1].reshape(rows, 256).astype(BF16))
        store(2 + mz, jnp.where(low1, form[2:], form[: n - 2]).reshape(rows, 256).astype(BF16))


def conv_lhs(before, here, after):
    parts = []
    for m in range(4):
        parts += [here[0][m, here[1]], after[0][m, after[1], :, :128], before[0][m, before[1], :, 128:]]
    return jnp.concatenate(parts, axis=1)


def coarse_forms(cells, store):
    n = cells.shape[0]
    for dz, form in enumerate((shift_z(cells, False), cells, shift_z(cells, True))):
        for dy in range(3):
            store(dy * 3 + dz, form[dy : dy + n - 2].reshape((n - 2) * 8, 128).astype(BF16))


def storer(scr, slot):
    def store(m, value):
        scr[m, slot] = value

    return store


def pair_lhs(low, high):
    parts = []
    for t in range(9):
        parts += [low[0][t, low[1]], high[0][t, high[1]]]
    return jnp.concatenate(parts, axis=1)


def spread_block(p_scr, slot, cells):
    mixed(cells.astype(F32).reshape(16, 8, 256), storer(p_scr, slot))


def forward_pair(places, marks, w1_ref, wd_ref, dv_scr, dv_slot, d_scr, d_slot):
    lhs = jnp.concatenate([conv_lhs(*places[:3]), conv_lhs(*places[1:])], axis=0)
    pre = dot(lhs, w1_ref[...])
    hidden = []
    for b in range(2):
        value, slope = silu_parts(pre[112 * b : 112 * b + 112])
        flags = jnp.concatenate([marks(b)] * 2, axis=1)
        hidden.append((flags * value).astype(BF16))
        dv_scr[dv_slot + b] = (flags * slope)[16:96]
    down = dot(jnp.concatenate(hidden, axis=1), wd_ref[...]).astype(BF16)
    coarse_forms(down.astype(F32).reshape(14, 8, 128), storer(d_scr, d_slot))
    return down


def coarse_forward(places, cots, w3_ref, g_scr, g_first):
    lhs = jnp.concatenate([pair_lhs(*places[:2]), pair_lhs(*places[1:])], axis=0)
    pre = dot(lhs, w3_ref[...])
    for k in range(2):
        _, slope = silu_parts(pre[96 * k : 96 * k + 96])
        grad = (cots(k).astype(F32) * slope).astype(BF16)
        coarse_forms(grad.astype(F32).reshape(12, 8, 128), storer(g_scr, g_first + k))


def fine_gradient(grad, slopes, wu_ref, q_scr, slot):
    for b in range(2):
        fine = (dot(grad, wu_ref[b]) * slopes(b)).astype(BF16)
        mixed(fine.astype(F32).reshape(10, 8, 256), storer(q_scr, slot + b))


def edge_kernel(
    flag_ref, own_ref, cown_ref, ya_ref, yb_ref, w1_ref, wd_ref,
    first_ref, second_ref, cot_ref, marks_ref, p_ref, dv_ref, d_ref,
    ext_ref, down_scr,
):
    odd_y, odd_x = is_odd("gy"), is_odd("gx")

    def place(above, below):
        for xb in range(NB):
            at = 48 * (xb // 2), 24 * (xb % 2)
            inner = [ref[pl.ds(at[0], 48), :].astype(F32)[at[1] : at[1] + 24] for ref in (above, below)]
            at = 192 + 16 * ((xb % 4) // 2), 8 * (xb % 2)
            outer = [ref[pl.ds(at[0], 16), :].astype(F32)[at[1] : at[1] + 8] for ref in (above, below)]
            if xb >= 4:
                outer = [pltpu.roll(outer[0], 64, 1), pltpu.roll(outer[1], 192, 1)]
            ext_ref[xb, pl.ds(0, 8), :] = outer[0]
            ext_ref[xb, pl.ds(8, 24), :] = inner[0]
            ext_ref[xb, pl.ds(32, 64), :] = own_ref[xb].astype(F32)
            ext_ref[xb, pl.ds(96, 24), :] = inner[1]
            ext_ref[xb, pl.ds(120, 8), :] = outer[1]
        for p in range(4):
            at = (pl.ds(224 + 16 * (p // 2), 16), pl.ds(128 * (p % 2), 128))
            cot_ref[p, pl.ds(0, 16), :] = above[at]
            cot_ref[p, pl.ds(16, 64), :] = cown_ref[p]
            cot_ref[p, pl.ds(80, 16), :] = below[at]
        for k in range(2):
            marks_ref[pl.ds(16 * k, 16), :] = above[pl.ds(256, 16), pl.ds(0, 128)]
            marks_ref[pl.ds(96 + 16 * k, 16), :] = below[pl.ds(256, 16), pl.ds(0, 128)]

    marks_ref[pl.ds(32, 64), :] = jnp.full((64, 128), flag_ref[0].astype(F32), F32).astype(BF16)
    pl.when(odd_y == 1)(lambda: place(yb_ref, ya_ref))
    pl.when(odd_y == 0)(lambda: place(ya_ref, yb_ref))

    marks = marks_ref[...].astype(F32)[8:120]
    for k in range(NB):
        spread_block(p_ref, k, ext_ref[k])
    for n in range(2):
        places = [(p_ref, 4 * n + k) for k in range(4)]
        down_scr[n] = forward_pair(places, lambda b: marks, w1_ref, wd_ref, dv_ref, 2 * n, d_ref, n)

    def send(low, high):
        for ref, n, near, outer, lane in ((low, 0, 0, 1, 0), (high, 1, 7, 6, 128)):
            ref[pl.ds(0, 128), :] = ext_ref[near].astype(BF16)
            for h in range(2):
                half = pl.ds(128 * h, 128)
                ref[pl.ds(128, 64), half] = ext_ref[outer, pl.ds(64 * h, 64), pl.ds(lane, 128)].astype(BF16)
                ref[pl.ds(192, 48), half] = cot_ref[3 * n, pl.ds(48 * h, 48), :]
            ref[pl.ds(240, 64), pl.ds(0, 128)] = down_scr[n, pl.ds(0, 64), :]
            ref[pl.ds(240, 48), pl.ds(128, 128)] = down_scr[n, pl.ds(64, 48), :]
            ends = [marks_ref[pl.ds(96 * k, 16), :].astype(F32)[:8] for k in range(2)]
            own = marks_ref[pl.ds(32, 16), :].astype(F32)
            flags = jnp.where(low_y((16, 128)), jnp.concatenate(ends, axis=0), own)
            ref[pl.ds(288, 16), pl.ds(128, 128)] = flags.astype(BF16)

    pl.when(odd_x == 1)(lambda: send(second_ref, first_ref))
    pl.when(odd_x == 0)(lambda: send(first_ref, second_ref))


def middle_kernel(
    cot_ref, marks_ref, p_ref, d_ref, w1_ref, w3_ref, w4_ref, wd_ref, wu_ref,
    g_ref, q_ref,
    dv_scr, d_scr,
):
    marks = marks_ref[...].astype(F32)[8:120]
    places = [(p_ref, 2 + k) for k in range(4)]
    forward_pair(places, lambda b: marks, w1_ref, wd_ref, dv_scr, 0, d_scr, 0)
    places = [(d_ref, 0), (d_scr, 0), (d_ref, 1)]
    coarse_forward(places, lambda k: cot_ref[1 + k], w3_ref, g_ref, 0)
    grad = dot(pair_lhs((g_ref, 0), (g_ref, 1)), w4_ref[...]).astype(BF16)
    fine_gradient(grad, lambda b: dv_scr[b], wu_ref, q_ref, 0)


def side_steps(
    side, msg_ref, cot_ref, marks_ref, pe_ref, dve_ref, de_ref, gm_ref, qm_ref, q_ref,
    w1_ref, w2_ref, w3_ref, w4_ref, wd_ref, wu_ref,
    store_out, scratch,
):
    p_scr, flag_scr, dv_scr, d_scr, cot_scr, g_scr, q_scr = scratch
    other = 1 - side
    right = side.astype(F32)

    spread_block(p_scr, 1 + side, msg_ref[pl.ds(0, 128), :])
    half = [msg_ref[pl.ds(128, 64), pl.ds(128 * h, 128)] for h in range(2)]
    half = jnp.concatenate(half, axis=0).astype(F32)
    spread_block(p_scr, 3 * side, jnp.concatenate([half * right, half * (1.0 - right)], axis=1))
    for k in range(2):
        for m in range(4):
            p_scr[m, 2 * other + k] = pe_ref[m, 6 * side + k]
        dv_scr[2 * other + k] = dve_ref[2 * side + k]
    flags = msg_ref[pl.ds(288, 16), pl.ds(128, 128)].astype(F32)
    turned = pltpu.roll(flags, 64, 1)
    ends = jnp.where(low_y((16, 128)), flags, turned)
    own = jnp.where(low_y((16, 128)), turned, flags)
    flag_scr[side] = jnp.concatenate([ends[:8]] * 3 + [own] * 4 + [ends[8:]] * 3, axis=0)
    flag_scr[other] = marks_ref[...].astype(F32)[8:120]
    for h in range(2):
        cot_scr[side, pl.ds(48 * h, 48), :] = msg_ref[pl.ds(192, 48), pl.ds(128 * h, 128)]
    cot_scr[other] = cot_ref[3 * side]
    down = [msg_ref[pl.ds(240, 64 - 16 * h), pl.ds(128 * h, 128)] for h in range(2)]
    down = jnp.concatenate(down, axis=0).astype(F32)
    coarse_forms(down.reshape(14, 8, 128), storer(d_scr, 2 * side))
    for t in range(9):
        d_scr[t, 2 * other] = de_ref[t, side]
        g_scr[t, 2 * other] = gm_ref[t, side]
    for m in range(4):
        for k in range(2):
            q_scr[m, 4 * other + k] = qm_ref[m, k]

    places = [(p_scr, k) for k in range(4)]
    forward_pair(places, lambda b: flag_scr[b], w1_ref, wd_ref, dv_scr, 2 * side, d_scr, 1)
    coarse_forward([(d_scr, k) for k in range(3)], lambda k: cot_scr[k], w3_ref, g_scr, side)
    lhs = jnp.concatenate([pair_lhs((g_scr, k), (g_scr, k + 1)) for k in range(2)], axis=0)
    grad = dot(lhs, w4_ref[...]).astype(BF16)
    for k in range(2):
        fine_gradient(grad[80 * k : 80 * k + 80], lambda b: dv_scr[2 * k + b], wu_ref, q_scr, 2 * side + 2 * k)
    lhs = jnp.concatenate([conv_lhs(*((q_scr, k + n) for n in range(3))) for k in range(4)], axis=0)
    grad = dot(lhs, w2_ref[...]).astype(BF16)
    lane = iota((32, 256), 1)
    low_y_cell, low_z_cell = (lane // 16) % 2 == 0, lane % 2 == 0
    for k in range(4):
        spread = lax.dot_general(grad[64 * k : 64 * k + 64], q_ref[...], TN, preferred_element_type=F32)
        for b in range(2):
            rows = [spread[128 * b + 32 * i : 128 * b + 32 * i + 32] for i in range(4)]
            pairs = [jnp.where(low_z_cell, rows[i], rows[i + 1]) for i in (0, 2)]
            store_out(2 * k + b, jnp.where(low_y_cell, *pairs))


def near_kernel(msg_ref, *refs):
    inputs, out_ref, scratch = refs[:14], refs[14], refs[15:]

    def store_out(x, rows):
        for h in range(2):
            out_ref[h, pl.ds(x, C1, stride=8), :] = rows[:, 128 * h : 128 * h + 128]

    side_steps(1 - is_odd("gx"), msg_ref, *inputs, store_out, scratch)


def far_kernel(msg_ref, near_ref, *refs):
    inputs, out_ref, scratch, o_scr = refs[:14], refs[14], refs[15:-1], refs[-1]
    side = is_odd("gx")
    o_scr[1 - side] = near_ref[...]

    def store_out(x, rows):
        for h in range(2):
            o_scr[side, h, pl.ds(x, C1, stride=8), :] = rows[:, 128 * h : 128 * h + 128]

    side_steps(side, msg_ref, *inputs, store_out, scratch)
    halves = [jnp.concatenate([o_scr[n, h].reshape(32, 8, 128) for h in range(2)], axis=2) for n in range(2)]
    out_ref[...] = jnp.concatenate(halves, axis=1).astype(BF16)


SIDE_SCRATCH = [
    pltpu.VMEM((4, 4, 112, 256), BF16),
    pltpu.VMEM((2, 112, 128), F32),
    pltpu.VMEM((4, 80, 256), F32),
    pltpu.VMEM((9, 3, 96, 128), BF16),
    pltpu.VMEM((2, 96, 128), BF16),
    pltpu.VMEM((9, 3, 80, 128), BF16),
    pltpu.VMEM((4, 6, 64, 256), BF16),
]
VMEM = pl.BlockSpec(memory_space=pltpu.VMEM)
SMEM = pl.BlockSpec(memory_space=pltpu.SMEM)


def call(kernel, specs, outs, scratch, flops, nbytes, *args):
    return pl.pallas_call(
        kernel,
        out_shape=outs,
        in_specs=specs,
        out_specs=jax.tree.map(lambda _: VMEM, outs),
        scratch_shapes=scratch,
        compiler_params=pltpu.CompilerParams(vmem_limit_bytes=24 * 1024 * 1024),
        cost_estimate=pl.CostEstimate(flops=flops, bytes_accessed=nbytes, transcendentals=0),
    )(*args)


def shape(*dims, dtype=BF16):
    return jax.ShapeDtypeStruct(dims, dtype)


def swaps(first, second, axis):
    count = lax.axis_size(axis)

    def both_ways(start):
        edges = [(i, i + 1) for i in range(start, count - 1, 2)]
        return edges + [(j, i) for i, j in edges]

    return lax.ppermute(first, axis, both_ways(1)), lax.ppermute(second, axis, both_ways(0))


def on_device(features, brick_mask, kernel_fine, kernel_down, kernel_coarse, cotangent):
    flag = brick_mask.reshape(1)
    q, parity = call(constant_kernel, [], [shape(64, 256), shape(256, 256)], [], 4 * 10**9, 10**5)
    own, cown, y_first, y_second = call(
        pack_kernel,
        [SMEM] + [VMEM] * 4,
        [shape(8, 64, 256), shape(4, 64, 128), shape(YMSG, 256), shape(YMSG, 256)],
        [pltpu.VMEM((2, 512, 128), F32), pltpu.VMEM((512, 128), F32), pltpu.VMEM((2, YMSG, 256), BF16)],
        2 * 10**9, 10**6, flag, features, cotangent, q, parity,
    )
    y_a, y_b = swaps(y_first, y_second, "gy")
    w1, w2, w3, w4, wd, wu = call(
        weight_kernel,
        [VMEM] * 3,
        [shape(2048, 256), shape(2048, 256), shape(2304, 128), shape(2304, 128), shape(512, 128), shape(2, 128, 256)],
        [
            pltpu.VMEM((27, 32, 256), BF16),
            pltpu.VMEM((36, 32, 256), BF16),
            pltpu.VMEM((48, 32, 256), BF16),
            pltpu.VMEM((27, 64, 128), BF16),
        ],
        10**9, 10**7,
        kernel_fine.reshape(27 * C1, C1),
        kernel_coarse.reshape(27 * C2, C2),
        kernel_down.reshape(8 * C2, C1),
    )
    x_first, x_second, cot, marks, pe, dve, de = call(
        edge_kernel,
        [SMEM] + [VMEM] * 6,
        [
            shape(XMSG, 256), shape(XMSG, 256), shape(4, 96, 128), shape(128, 128),
            shape(4, 8, 112, 256), shape(4, 80, 256, dtype=F32), shape(9, 2, 96, 128),
        ],
        [pltpu.VMEM((8, 128, 256), F32), pltpu.VMEM((2, 112, 128), BF16)],
        5 * 10**8, 10**6, flag, own, cown, y_a, y_b, w1, wd,
    )
    x_a, x_b = swaps(x_first, x_second, "gx")
    gm, qm = call(
        middle_kernel,
        [VMEM] * 9,
        [shape(9, 2, 80, 128), shape(4, 2, 64, 256)],
        [pltpu.VMEM((2, 80, 256), F32), pltpu.VMEM((9, 1, 96, 128), BF16)],
        2 * 10**10, 10**7,
        cot, marks, pe, de, w1, w3, w4, wd, wu,
    )
    shared = (cot, marks, pe, dve, de, gm, qm, q, w1, w2, w3, w4, wd, wu)
    near = call(
        near_kernel,
        [VMEM] * 15,
        shape(2, 256, 128, dtype=F32),
        SIDE_SCRATCH,
        2 * 10**10, 10**7, x_b, *shared,
    )
    return call(
        far_kernel,
        [VMEM] * 16,
        shape(32, 16, 256),
        SIDE_SCRATCH + [pltpu.VMEM((2, 2, 256, 128), F32)],
        10**10, 10**7, x_a, near, *shared,
    )


def solution(mesh):
    placed = (P(None, "gx", "gy"), P("gx", "gy", None), P(), P(), P(), P(None, "gx", "gy"))
    return jax.shard_map(
        on_device, mesh=mesh, in_specs=placed, out_specs=P(None, "gx", "gy"), check_vma=False
    )
```
